512 devices in a mesh: rx: 32 (over z, x), ry: 16 (over y, core).
Axes of the slice: x: 4, y: 8, z: 8, core: 2. Of those that a mesh axis runs over, the one named last changes fastest.
Arguments:
- start_block: bfloat16 [64, 524288], P(None, ('rx', 'ry')), may hold values from -0.4 to 0.4
- operator_tiles: bfloat16 [4096, 8, 128, 128], P(('rx', 'ry')), may hold values from -0.125 to 0.125
- tile_pattern: int32 [4096, 8], P(('rx', 'ry')), may hold values from 0 to 4095, as said below
Outputs:
- basis_block: float32 [64, 524288], P(None, ('rx', 'ry'))
- factor: float32 [64, 64], replicated
The draws below stay inside these ranges and needn't reach their ends.
Inputs may be any that keep to these rules, and one draw needn't show every extreme that they name: `tile_pattern`: entry [i, 0] is i. Every entry j of row i has |j - i| <= 16. Entries 1 and 2 of row i are i - 16 and i + 16, reflected at the ends of the range. A row may name a column more than once.
All inputs are finite; a program needn't handle non-finite values.
Results may differ from the reference program's by a relative error of at most 0.015.
Values may be sent and summed in bfloat16 or wider, within the bound.
No kernel may reach another device: no remote copies, remote signals or barrier semaphores. Data moves between devices by JAX's collectives and lax.ppermute only.
A program may use at most 64 MiB of HBM per device.

```python
import math
import jax
import jax.numpy as jnp
from jax import lax

TILE = 128
NV = 64
TILE_ROWS_DEV = 8
SLOTS = 8
SPAN = 2
DEG = 12
TILE_ROWS = 4096
NODES = 524288
N_RX = 32
N_RY = 16


def draw_start_block(key, part):
    key = jax.random.fold_in(key, 11)
    keys = jax.random.split(key, 3)
    row_scale = jnp.exp(jax.random.uniform(keys[1], (1, NODES), jnp.float32) * math.log(10.0))
    column_scale = jnp.exp(jax.random.uniform(keys[2], (NV, 1), jnp.float32) * math.log(10.0))
    base = jnp.clip(jax.random.normal(keys[0], (NV, NODES), jnp.float32), -4.0, 4.0)
    return (base * row_scale * column_scale / 1000.0).astype(jnp.bfloat16)


def draw_tile_pattern(key, part):
    key = jax.random.fold_in(key, 5)
    reach_tiles = SPAN * TILE_ROWS_DEV
    row_ids = jnp.arange(TILE_ROWS, dtype=jnp.int32)[:, None]
    random_offsets = jax.random.randint(key, (TILE_ROWS, SLOTS - 3), -reach_tiles, reach_tiles + 1, dtype=jnp.int32)
    fixed_offsets = jnp.broadcast_to(jnp.array([0, -reach_tiles, reach_tiles], jnp.int32)[None, :], (TILE_ROWS, 3))
    columns = row_ids + jnp.concatenate([fixed_offsets, random_offsets], axis=1)
    columns = jnp.where(columns < 0, -columns, columns)
    columns = jnp.where(columns > TILE_ROWS - 1, 2 * (TILE_ROWS - 1) - columns, columns)
    return columns.astype(jnp.int32)


def block_scale(stream_key, extent, cuts, low, largest):
    level, own = 1.0, jax.random.fold_in(stream_key, 6)
    for axis_at, blocks in cuts:
        draws = jnp.exp(jax.random.uniform(jax.random.fold_in(own, axis_at), (blocks,), jnp.float32, low / len(cuts), largest / len(cuts)))
        level = level * jnp.repeat(draws, extent[axis_at] // blocks).reshape([-1 if axis == axis_at else 1 for axis in range(len(extent))])
    return level


def normal_values(own_key, shape, deviation, most, shards=(), held_as=jnp.bfloat16):
    drawn = deviation * jax.random.normal(own_key, shape, jnp.float32)
    if shards:
        drawn = drawn * block_scale(own_key, shape, shards, -0.22, 0.18)
    return jnp.clip(drawn, -most, most).astype(held_as)


def setup_inputs(seed: int = 0) -> dict:
    streams_of = jax.random.split(jax.random.key(seed), 4)
    return {
        "start_block": draw_start_block(jax.random.fold_in(streams_of[3], 71), 0),
        "operator_tiles": normal_values(streams_of[1], (TILE_ROWS, SLOTS, TILE, TILE), (2 * SLOTS * TILE) ** -0.5, 0.125, ((0, 512),)),
        "tile_pattern": draw_tile_pattern(jax.random.fold_in(streams_of[3], 71), 0),
    }


def apply_operator(vectors, operator_tiles, tile_pattern):
    vector_tiles = vectors.astype(jnp.float32).reshape(NV, TILE_ROWS, TILE)
    blocks = N_RX * N_RY
    tile_blocks = operator_tiles.reshape(blocks, TILE_ROWS_DEV, SLOTS, TILE, TILE)
    pattern_blocks = tile_pattern.reshape(blocks, TILE_ROWS_DEV, SLOTS)

    def one_block(block_pair):
        block_tiles, block_pattern = block_pair
        picked = jnp.take(vector_tiles, block_pattern, axis=1)
        return jnp.einsum('vrkt,rkst->vrs', picked, block_tiles.astype(jnp.float32), precision=lax.Precision.HIGHEST)
    result = lax.map(one_block, (tile_blocks, pattern_blocks))
    return jnp.transpose(result, (1, 0, 2, 3)).reshape(NV, NODES)

def reference(start_block, operator_tiles, tile_pattern):
    earlier = start_block.astype(jnp.float32)
    current = apply_operator(start_block, operator_tiles, tile_pattern)
    for round_index in range(DEG - 1):
        following = 2.0 * apply_operator(current.astype(jnp.bfloat16), operator_tiles, tile_pattern) - earlier
        earlier, current = (current, following)
    q_part, r_part = jnp.linalg.qr(current.T)
    sign_flip = jnp.sign(jnp.diagonal(r_part))
    root_nodes = jnp.sqrt(jnp.float32(NODES))
    factor = r_part * sign_flip[:, None] / root_nodes
    basis_block = (q_part * sign_flip[None, :]).T * root_nodes
    return (basis_block, factor)
```

```python
import functools

import jax
import jax.numpy as jnp
from jax import lax
from jax.experimental import pallas as pl
from jax.experimental.pallas import tpu as pltpu
from jax.sharding import PartitionSpec as P

DEG = 12
AXES = ("rx", "ry")
VMEM = pl.BlockSpec(memory_space=pltpu.VMEM)
SMEM = pl.BlockSpec(memory_space=pltpu.SMEM)
LIMIT = 32 * 2**20


def moved(value, steps):
    count = lax.axis_size(AXES)
    first, last = max(0, -steps), min(count, count - steps)
    return lax.ppermute(value, AXES, [(source, source + steps) for source in range(first, last)])


def swapped(value):
    count = lax.axis_size(AXES)
    return lax.ppermute(value, AXES, [(source, source ^ 1) for source in range(count)])


def turn_kernel(tiles_ref, out_ref):
    rows, slots = tiles_ref.shape[:2]
    for row in range(rows):
        for slot in range(slots):
            out_ref[row, slot] = tiles_ref[row, slot].T


def turned(tiles):
    return pl.pallas_call(
        turn_kernel,
        in_specs=[VMEM],
        out_specs=VMEM,
        out_shape=jax.ShapeDtypeStruct(tiles.shape, tiles.dtype),
        compiler_params=pltpu.CompilerParams(vmem_limit_bytes=LIMIT),
        name="turn_tiles",
    )(tiles)


def step_kernel(first, index_ref, left_ref, own_ref, right_ref, near_ref, far_ref, *rest):
    older_ref, latest_ref, rounded_ref, window = (None, *rest) if first else rest
    count = own_ref.shape[0]
    window[0:count] = left_ref[...]
    window[count : 2 * count] = own_ref[...]
    window[2 * count : 3 * count] = right_ref[...]
    half, slots = near_ref.shape[:2]
    for row in range(count):
        tiles_ref, at = (near_ref, row) if row < half else (far_ref, row - half)
        total = None
        for slot in range(0, slots, 2):
            vectors = jnp.concatenate(
                [window[index_ref[row, slot]], window[index_ref[row, slot + 1]]], axis=1
            )
            tiles = jnp.concatenate([tiles_ref[at, slot], tiles_ref[at, slot + 1]], axis=0)
            part = jnp.dot(vectors, tiles, preferred_element_type=jnp.float32)
            total = part if total is None else total + part
        if not first:
            total = 2.0 * total - older_ref[row]
        latest_ref[row] = total
        rounded_ref[row] = total.astype(jnp.bfloat16)


def step(index, left, own, right, near, far, older=None):
    first = older is None
    flops = 2 * own.size * own.shape[2] * near.shape[1]
    return pl.pallas_call(
        functools.partial(step_kernel, first),
        in_specs=[SMEM] + [VMEM] * (5 if first else 6),
        out_specs=[VMEM, VMEM],
        out_shape=[
            jax.ShapeDtypeStruct(own.shape, jnp.float32),
            jax.ShapeDtypeStruct(own.shape, jnp.bfloat16),
        ],
        scratch_shapes=[pltpu.VMEM((3 * own.shape[0],) + own.shape[1:], jnp.bfloat16)],
        compiler_params=pltpu.CompilerParams(vmem_limit_bytes=LIMIT),
        cost_estimate=pl.CostEstimate(flops=flops, bytes_accessed=4 * near.size, transcendentals=0),
        name="first_step" if first else "step",
    )(index, left, own, right, near, far, *(() if first else (older,)))


def gram_kernel(scale, core_ref, mine_ref, theirs_ref, block_ref, gram_ref):
    tiles, half, width = mine_ref.shape
    even = core_ref[0] == 0
    for tile in range(tiles):
        mine, theirs = mine_ref[tile], theirs_ref[tile]
        columns = pl.ds(tile * width, width)
        block_ref[0:half, columns] = jnp.where(even, mine, theirs)
        block_ref[half : 2 * half, columns] = jnp.where(even, theirs, mine)
    block = block_ref[...]
    gram_ref[...] = scale * lax.dot_general(
        block,
        block,
        (((1,), (1,)), ((), ())),
        precision=lax.Precision.HIGHEST,
        preferred_element_type=jnp.float32,
    )


def gram_of(core, mine, theirs, scale):
    tiles, half, width = mine.shape
    return pl.pallas_call(
        functools.partial(gram_kernel, scale),
        in_specs=[SMEM, VMEM, VMEM],
        out_specs=[VMEM, VMEM],
        out_shape=[
            jax.ShapeDtypeStruct((2 * half, tiles * width), jnp.float32),
            jax.ShapeDtypeStruct((2 * half, 2 * half), jnp.float32),
        ],
        compiler_params=pltpu.CompilerParams(vmem_limit_bytes=LIMIT),
        name="gram",
    )(core, mine, theirs)


def finish_kernel(gram_ref, block_ref, basis_ref, factor_ref, rows):
    size = gram_ref.shape[0]
    row_of = lax.broadcasted_iota(jnp.int32, (8, 2 * size), 0)
    lane_of = lax.broadcasted_iota(jnp.int32, (8, 2 * size), 1)
    groups = []
    for group in range(size // 8):
        unit = (lane_of == row_of + (8 * group + size)).astype(jnp.float32)
        groups.append(
            jnp.concatenate([gram_ref[8 * group : 8 * group + 8, :], unit[:, size:]], axis=1)
        )
    for pivot in range(size):
        at, inner = divmod(pivot, 8)
        pivot_row = groups[at][inner : inner + 1, :]
        diagonal = pivot_row[:, pivot : pivot + 1]
        rows[pivot : pivot + 1, :] = pivot_row * lax.rsqrt(diagonal)
        scaled = pivot_row * (1.0 / diagonal)
        for group in range(at, size // 8):
            column = groups[group][:, pivot : pivot + 1]
            if group == at:
                if inner == 7:
                    continue
                column = jnp.where(row_of[:, :1] > inner, column, 0.0)
            groups[group] = groups[group] - column * scaled
    upper = lax.broadcasted_iota(jnp.int32, (size, size), 0) <= lax.broadcasted_iota(
        jnp.int32, (size, size), 1
    )
    done = rows[...]
    factor_ref[...] = jnp.where(upper, done[:, :size], 0.0)
    basis_ref[...] = jnp.dot(
        done[:, size:],
        block_ref[...],
        precision=lax.Precision.HIGHEST,
        preferred_element_type=jnp.float32,
    )


def finish(gram, block):
    size = gram.shape[0]
    return pl.pallas_call(
        finish_kernel,
        in_specs=[VMEM, VMEM],
        out_specs=[VMEM, VMEM],
        out_shape=[
            jax.ShapeDtypeStruct(block.shape, jnp.float32),
            jax.ShapeDtypeStruct(gram.shape, jnp.float32),
        ],
        scratch_shapes=[pltpu.VMEM((size, 2 * size), jnp.float32)],
        compiler_params=pltpu.CompilerParams(vmem_limit_bytes=LIMIT),
        name="factor_and_solve",
    )(gram, block)


def summed(gram):
    size = gram.shape[0]
    inner, outer = lax.axis_size("ry"), lax.axis_size("rx")
    part = lax.all_to_all(gram.reshape(inner, size // inner * size), "ry", 0, 0, tiled=True)
    part = jnp.sum(part, axis=0)
    part = lax.all_to_all(jnp.broadcast_to(part, (outer,) + part.shape), "rx", 0, 0, tiled=True)
    part = jnp.sum(part, axis=0)
    part = lax.all_to_all(jnp.broadcast_to(part, (inner,) + part.shape), "ry", 0, 0, tiled=True)
    return part.reshape(size, size)


def shards(start_block, operator_tiles, tile_pattern):
    vectors, node_count = start_block.shape
    rows_local, _, tile_size = operator_tiles.shape[:3]
    half = vectors // 2
    device_count = lax.axis_size(AXES)
    position = lax.axis_index(AXES)
    core = position % 2
    chip_rows = 2 * rows_local

    start_tiles = start_block.reshape(vectors, rows_local, tile_size).transpose(1, 0, 2)
    low, high = start_tiles[:, :half], start_tiles[:, half:]
    mine = jnp.where(core == 0, low, high)
    theirs = swapped(jnp.where(core == 0, high, low))
    rounded = jnp.concatenate([mine, theirs], axis=0)

    near = turned(operator_tiles)
    far = swapped(near)
    pattern = jnp.concatenate([tile_pattern, swapped(tile_pattern)], axis=0)
    index = jnp.clip(pattern - (position // 2 - 1) * chip_rows, 0, 3 * chip_rows - 1)
    index = index ^ (core * rows_local)

    earlier = rounded.astype(jnp.float32)
    latest, rounded = step(index, moved(rounded, 2), rounded, moved(rounded, -2), near, far)
    for _ in range(DEG - 1):
        following, next_rounded = step(
            index, moved(rounded, 2), rounded, moved(rounded, -2), near, far, earlier
        )
        earlier, latest, rounded = latest, following, next_rounded

    block, gram = gram_of(
        core.reshape(1),
        latest[:rows_local],
        swapped(latest[rows_local:]),
        1.0 / (node_count * device_count),
    )
    return finish(summed(gram), block)


def solution(mesh):
    return jax.shard_map(
        shards,
        mesh=mesh,
        in_specs=(P(None, AXES), P(AXES, None, None, None), P(AXES, None)),
        out_specs=(P(None, AXES), P()),
        check_vma=False,
    )
```

```python
import functools

import jax
import jax.numpy as jnp
from jax import lax
from jax.experimental import pallas as pl
from jax.experimental.pallas import tpu as pltpu
from jax.sharding import PartitionSpec as P

DEG = 12
AXES = ("rx", "ry")
VMEM = pl.BlockSpec(memory_space=pltpu.VMEM)
SMEM = pl.BlockSpec(memory_space=pltpu.SMEM)
LIMIT = 16 * 2**20


def traded(value, first):
    count = lax.axis_size(AXES)
    route = []
    for low in range(2 * first, count - 2, 4):
        for core in (0, 1):
            route += [(low + core, low + core + 2), (low + core + 2, low + core)]
    return lax.ppermute(value, AXES, route)


def swapped(value):
    count = lax.axis_size(AXES)
    return lax.ppermute(value, AXES, [(source, source ^ 1) for source in range(count)])


def turn_kernel(near_ref, far_ref, out_ref):
    rows, slots = near_ref.shape[:2]
    for row in range(rows):
        for slot in range(slots):
            out_ref[row, slot] = near_ref[row, slot].T
            out_ref[rows + row, slot] = far_ref[row, slot].T


def turned(near, far):
    return pl.pallas_call(
        turn_kernel,
        in_specs=[VMEM, VMEM],
        out_specs=VMEM,
        out_shape=jax.ShapeDtypeStruct((2 * near.shape[0],) + near.shape[1:], near.dtype),
        compiler_params=pltpu.CompilerParams(vmem_limit_bytes=LIMIT),
        name="turn_tiles",
    )(near, far)


def step_kernel(first, index_ref, even_ref, own_ref, odd_ref, tiles_ref, *rest):
    older_ref, latest_ref, rounded_ref, window = (None, *rest) if first else rest
    count = own_ref.shape[0]
    window[0:count] = odd_ref[...]
    window[count : 2 * count] = own_ref[...]
    window[2 * count : 3 * count] = even_ref[...]
    slots = tiles_ref.shape[1]
    for row in range(count):
        total = None
        for slot in range(0, slots, 2):
            vectors = jnp.concatenate(
                [window[index_ref[row, slot]], window[index_ref[row, slot + 1]]], axis=1
            )
            tiles = jnp.concatenate([tiles_ref[row, slot], tiles_ref[row, slot + 1]], axis=0)
            part = jnp.dot(vectors, tiles, preferred_element_type=jnp.float32)
            total = part if total is None else total + part
        if not first:
            total = 2.0 * total - older_ref[row]
        latest_ref[row] = total
        rounded_ref[row] = total.astype(jnp.bfloat16)


def step(index, even, own, odd, tiles, older=None):
    first = older is None
    flops = 2 * own.size * own.shape[2] * tiles.shape[1]
    return pl.pallas_call(
        functools.partial(step_kernel, first),
        in_specs=[SMEM] + [VMEM] * (4 if first else 5),
        out_specs=[VMEM, VMEM],
        out_shape=[
            jax.ShapeDtypeStruct(own.shape, jnp.float32),
            jax.ShapeDtypeStruct(own.shape, jnp.bfloat16),
        ],
        scratch_shapes=[pltpu.VMEM((3 * own.shape[0],) + own.shape[1:], jnp.bfloat16)],
        compiler_params=pltpu.CompilerParams(vmem_limit_bytes=LIMIT),
        cost_estimate=pl.CostEstimate(flops=flops, bytes_accessed=2 * tiles.size, transcendentals=0),
        name="first_step" if first else "step",
    )(index, even, own, odd, tiles, *(() if first else (older,)))


def gram_kernel(scale, core_ref, mine_ref, theirs_ref, block_ref, gram_ref):
    tiles, half, width = mine_ref.shape
    even = core_ref[0] == 0
    for tile in range(tiles):
        mine, theirs = mine_ref[tile], theirs_ref[tile]
        columns = pl.ds(tile * width, width)
        block_ref[0:half, columns] = jnp.where(even, mine, theirs)
        block_ref[half : 2 * half, columns] = jnp.where(even, theirs, mine)
    block = block_ref[...]
    gram_ref[...] = scale * lax.dot_general(
        block,
        block,
        (((1,), (1,)), ((), ())),
        precision=lax.Precision.HIGHEST,
        preferred_element_type=jnp.float32,
    )


def gram_of(core, mine, theirs, scale):
    tiles, half, width = mine.shape
    return pl.pallas_call(
        functools.partial(gram_kernel, scale),
        in_specs=[SMEM, VMEM, VMEM],
        out_specs=[VMEM, VMEM],
        out_shape=[
            jax.ShapeDtypeStruct((2 * half, tiles * width), jnp.float32),
            jax.ShapeDtypeStruct((2 * half, 2 * half), jnp.float32),
        ],
        compiler_params=pltpu.CompilerParams(vmem_limit_bytes=LIMIT),
        name="gram",
    )(core, mine, theirs)


def finish_kernel(gram_ref, block_ref, basis_ref, factor_ref, rows):
    size = gram_ref.shape[0]
    row_of = lax.broadcasted_iota(jnp.int32, (8, 2 * size), 0)
    lane_of = lax.broadcasted_iota(jnp.int32, (8, 2 * size), 1)
    groups = []
    for group in range(size // 8):
        unit = (lane_of == row_of + (8 * group + size)).astype(jnp.float32)
        groups.append(
            jnp.concatenate([gram_ref[8 * group : 8 * group + 8, :], unit[:, size:]], axis=1)
        )
    for pivot in range(size):
        at, inner = divmod(pivot, 8)
        pivot_row = groups[at][inner : inner + 1, :]
        diagonal = pivot_row[:, pivot : pivot + 1]
        rows[pivot : pivot + 1, :] = pivot_row * lax.rsqrt(diagonal)
        scaled = pivot_row * (1.0 / diagonal)
        for group in range(at, size // 8):
            column = groups[group][:, pivot : pivot + 1]
            if group == at:
                if inner == 7:
                    continue
                column = jnp.where(row_of[:, :1] > inner, column, 0.0)
            groups[group] = groups[group] - column * scaled
    upper = lax.broadcasted_iota(jnp.int32, (size, size), 0) <= lax.broadcasted_iota(
        jnp.int32, (size, size), 1
    )
    done = rows[...]
    factor_ref[...] = jnp.where(upper, done[:, :size], 0.0)
    basis_ref[...] = jnp.dot(
        done[:, size:],
        block_ref[...],
        precision=lax.Precision.HIGHEST,
        preferred_element_type=jnp.float32,
    )


def finish(gram, block):
    size = gram.shape[0]
    return pl.pallas_call(
        finish_kernel,
        in_specs=[VMEM, VMEM],
        out_specs=[VMEM, VMEM],
        out_shape=[
            jax.ShapeDtypeStruct(block.shape, jnp.float32),
            jax.ShapeDtypeStruct(gram.shape, jnp.float32),
        ],
        scratch_shapes=[pltpu.VMEM((size, 2 * size), jnp.float32)],
        compiler_params=pltpu.CompilerParams(vmem_limit_bytes=LIMIT),
        name="factor_and_solve",
    )(gram, block)


def summed(gram):
    size = gram.shape[0]
    inner, outer = lax.axis_size("ry"), lax.axis_size("rx")
    part = lax.all_to_all(gram.reshape(inner, size // inner * size), "ry", 0, 0, tiled=True)
    part = jnp.sum(part, axis=0)
    part = lax.all_to_all(jnp.broadcast_to(part, (outer,) + part.shape), "rx", 0, 0, tiled=True)
    part = jnp.sum(part, axis=0)
    part = lax.all_to_all(jnp.broadcast_to(part, (inner,) + part.shape), "ry", 0, 0, tiled=True)
    return part.reshape(size, size)


def shards(start_block, operator_tiles, tile_pattern):
    vectors, node_count = start_block.shape
    rows_local, _, tile_size = operator_tiles.shape[:3]
    half = vectors // 2
    device_count = lax.axis_size(AXES)
    position = lax.axis_index(AXES)
    chip, core = position // 2, position % 2
    chip_rows = 2 * rows_local

    row_ids = jnp.arange(rows_local, dtype=jnp.int32)[:, None]
    away = tile_pattern - (position * rows_local + row_ids)
    start_tiles = start_block.reshape(vectors, rows_local, tile_size).transpose(1, 0, 2)
    low, high = start_tiles[:, :half], start_tiles[:, half:]
    slots = away.shape[1]
    packed = jnp.zeros((1, half, tile_size), jnp.bfloat16)
    packed = packed.at[0, :rows_local, :slots].set(away.astype(jnp.bfloat16))
    theirs = swapped(jnp.concatenate([jnp.where(core == 0, high, low), packed], axis=0))
    rounded = jnp.concatenate([jnp.where(core == 0, low, high), theirs[:rows_local]], axis=0)
    far_away = theirs[rows_local, :rows_local, :slots].astype(jnp.int32)

    tiles = turned(operator_tiles, swapped(operator_tiles))

    far_rows = (position ^ 1) * rows_local + row_ids
    columns = jnp.concatenate([tile_pattern, far_away + far_rows], axis=0)
    index = jnp.clip(columns - (chip - 1) * chip_rows, 0, 3 * chip_rows - 1)
    place, inner = index // chip_rows, (index % chip_rows) ^ (core * rows_local)
    index = jnp.where(chip % 2 == 1, 2 - place, place) * chip_rows + inner

    def neighbours(own):
        odd = traded(own, 1)
        even = traded(own, 0)
        return even, own, odd

    earlier = rounded.astype(jnp.float32)
    latest, rounded = step(index, *neighbours(rounded), tiles)
    for _ in range(DEG - 1):
        following, next_rounded = step(index, *neighbours(rounded), tiles, earlier)
        earlier, latest, rounded = latest, following, next_rounded

    block, gram = gram_of(
        core.reshape(1),
        latest[:rows_local],
        swapped(latest[rows_local:]),
        1.0 / (node_count * device_count),
    )
    return finish(summed(gram), block)


def solution(mesh):
    return jax.shard_map(
        shards,
        mesh=mesh,
        in_specs=(P(None, AXES), P(AXES, None, None, None), P(AXES, None)),
        out_specs=(P(None, AXES), P()),
        check_vma=False,
    )
```

```python
import functools

import jax
import jax.numpy as jnp
from jax import lax
from jax.experimental import pallas as pl
from jax.experimental.pallas import tpu as pltpu
from jax.sharding import PartitionSpec as P

DEG = 12
AXES = ("rx", "ry")
VMEM = pl.BlockSpec(memory_space=pltpu.VMEM)
SMEM = pl.BlockSpec(memory_space=pltpu.SMEM)
LIMIT = 16 * 2**20


def traded(value, first):
    count = lax.axis_size(AXES)
    route = []
    for low in range(2 * first, count - 2, 4):
        for core in (0, 1):
            route += [(low + core, low + core + 2), (low + core + 2, low + core)]
    return lax.ppermute(value, AXES, route)


def paired(value):
    groups = []
    for low in range(0, lax.axis_size("ry"), 4):
        groups += [[low, low + 2], [low + 1, low + 3]]
    return lax.all_gather(value, "ry", axis_index_groups=groups)


def of_both_cores(value):
    count = lax.axis_size("ry")
    groups = [[low, low + 1] for low in range(0, count, 2)]
    return lax.all_gather(value, "ry", axis_index_groups=groups)


def swapped(value):
    count = lax.axis_size(AXES)
    return lax.ppermute(value, AXES, [(source, source ^ 1) for source in range(count)])


def turn_kernel(near_ref, far_ref, out_ref):
    rows, slots = near_ref.shape[:2]
    for row in range(rows):
        for slot in range(slots):
            out_ref[row, slot] = near_ref[row, slot].T
            out_ref[rows + row, slot] = far_ref[row, slot].T


def turned(near, far):
    return pl.pallas_call(
        turn_kernel,
        in_specs=[VMEM, VMEM],
        out_specs=VMEM,
        out_shape=jax.ShapeDtypeStruct((2 * near.shape[0],) + near.shape[1:], near.dtype),
        compiler_params=pltpu.CompilerParams(vmem_limit_bytes=LIMIT),
        name="turn_tiles",
    )(near, far)


def apply_tiles(index_ref, tiles_ref, window, older_ref, latest_ref, rounded_ref):
    count, slots = tiles_ref.shape[:2]
    for row in range(count):
        total = None
        for slot in range(0, slots, 2):
            vectors = jnp.concatenate(
                [window[index_ref[row, slot]], window[index_ref[row, slot + 1]]], axis=1
            )
            tiles = jnp.concatenate([tiles_ref[row, slot], tiles_ref[row, slot + 1]], axis=0)
            part = jnp.dot(vectors, tiles, preferred_element_type=jnp.float32)
            total = part if total is None else total + part
        if older_ref is not None:
            total = 2.0 * total - older_ref[row]
        if latest_ref is not None:
            latest_ref[row] = total
        if rounded_ref is not None:
            rounded_ref[row] = total.astype(jnp.bfloat16)


def first_kernel(
    index_ref, even_chip_ref, even_ref, own_ref, odd_ref, tiles_ref, latest_ref, rounded_ref, window
):
    count = odd_ref.shape[0]
    is_even = even_chip_ref[0] == 1
    own, even = own_ref[...], even_ref[...]
    window[0:count] = odd_ref[...]
    window[count : 2 * count] = jnp.where(is_even, own, even)
    window[2 * count : 3 * count] = jnp.where(is_even, even, own)
    apply_tiles(index_ref, tiles_ref, window, None, latest_ref, rounded_ref)


def step_kernel(keep, index_ref, pair_ref, odd_ref, tiles_ref, older_ref, *rest):
    latest_ref = rest[0] if keep[0] else None
    rounded_ref = rest[-2] if keep[1] else None
    window = rest[-1]
    count = odd_ref.shape[0]
    window[0:count] = odd_ref[...]
    window[count : 2 * count] = pair_ref[0]
    window[2 * count : 3 * count] = pair_ref[1]
    apply_tiles(index_ref, tiles_ref, window, older_ref, latest_ref, rounded_ref)


def stepped(kernel, name, scalars, blocks, keep=(True, True)):
    tiles = next(block for block in blocks if block.ndim == 4 and block.shape[-2] == block.shape[-1])
    shape = (tiles.shape[0], blocks[0].shape[-2], tiles.shape[2])
    kinds = [kind for kind, kept in zip((jnp.float32, jnp.bfloat16), keep) if kept]
    return pl.pallas_call(
        kernel,
        in_specs=[SMEM] * len(scalars) + [VMEM] * len(blocks),
        out_specs=[VMEM] * len(kinds),
        out_shape=[jax.ShapeDtypeStruct(shape, kind) for kind in kinds],
        scratch_shapes=[pltpu.VMEM((3 * shape[0],) + shape[1:], jnp.bfloat16)],
        compiler_params=pltpu.CompilerParams(vmem_limit_bytes=LIMIT),
        cost_estimate=pl.CostEstimate(
            flops=2 * shape[1] * tiles.size, bytes_accessed=2 * tiles.size, transcendentals=0
        ),
        name=name,
    )(*scalars, *blocks)


def gram_kernel(scale, core_ref, mine_ref, both_ref, block_ref, part_ref, wide):
    tiles, half, width = mine_ref.shape
    core = core_ref[0]
    even = core == 0
    for tile in range(tiles):
        mine, theirs = mine_ref[tile], both_ref[1 - core, (tile + tiles // 2) % tiles]
        columns = pl.ds(tile * width, width)
        wide[0:half, columns] = jnp.where(even, mine, theirs)
        wide[half : 2 * half, columns] = jnp.where(even, theirs, mine)
    block_ref[...] = wide[:, : tiles // 2 * width]
    mine = jnp.concatenate([mine_ref[tile] for tile in range(tiles)], axis=1)
    part = scale * lax.dot_general(
        mine,
        wide[...],
        (((1,), (1,)), ((), ())),
        precision=lax.Precision.HIGHEST,
        preferred_element_type=jnp.float32,
    )
    part = jnp.concatenate([part[: half // 2], part[half // 2 :]], axis=1)
    part_ref[...] = jnp.broadcast_to(part[None], part_ref.shape)


def gram_rows(core, mine, both, scale, copies):
    tiles, half, width = mine.shape
    return pl.pallas_call(
        functools.partial(gram_kernel, scale),
        in_specs=[SMEM, VMEM, VMEM],
        out_specs=[VMEM, VMEM],
        out_shape=[
            jax.ShapeDtypeStruct((2 * half, tiles // 2 * width), jnp.float32),
            jax.ShapeDtypeStruct((copies, half // 2, 4 * half), jnp.float32),
        ],
        scratch_shapes=[pltpu.VMEM((2 * half, tiles * width), jnp.float32)],
        compiler_params=pltpu.CompilerParams(vmem_limit_bytes=LIMIT),
        name="gram",
    )(core, mine, both)


def sum_kernel(parts_ref, out_ref):
    parts = [parts_ref[at] for at in range(parts_ref.shape[0])]
    while len(parts) > 1:
        parts = [one + other for one, other in zip(parts[::2], parts[1::2])]
    out_ref[...] = jnp.broadcast_to(parts[0][None], out_ref.shape)


def summed(parts, copies):
    return pl.pallas_call(
        sum_kernel,
        in_specs=[VMEM],
        out_specs=VMEM,
        out_shape=jax.ShapeDtypeStruct((copies,) + parts.shape[1:], parts.dtype),
        compiler_params=pltpu.CompilerParams(vmem_limit_bytes=LIMIT),
        name="sum_parts",
    )(parts)


def finish_kernel(gram_ref, block_ref, basis_ref, factor_ref, rows):
    size = block_ref.shape[0]
    quarter = size // 4
    lane_of = lax.broadcasted_iota(jnp.int32, (8, 2 * size), 1)
    row_of = lax.broadcasted_iota(jnp.int32, (8, 2 * size), 0)
    groups = []
    for group in range(size // 8):
        core, row = divmod(8 * group, 2 * quarter)
        part, row = divmod(row, quarter)
        stored = gram_ref[core, row : row + 8, part * size : (part + 1) * size]
        unit = (lane_of == row_of + (8 * group + size)).astype(jnp.float32)
        groups.append(jnp.concatenate([stored, unit[:, size:]], axis=1))
    def spread(value):
        return jnp.broadcast_to(value, (8, 2 * size))

    for pivot in range(0, size, 2):
        at, inner = divmod(pivot, 8)
        own = groups[at]
        one, two = spread(own[inner : inner + 1, :]), spread(own[inner + 1 : inner + 2, :])
        firsts = [spread(group[:, pivot : pivot + 1]) for group in groups[at:]]
        seconds = [spread(group[:, pivot + 1 : pivot + 2]) for group in groups[at:]]
        corner, off = spread(firsts[0][inner : inner + 1, :]), spread(seconds[0][inner : inner + 1, :])
        other = spread(seconds[0][inner + 1 : inner + 2, :])
        inverse = 1.0 / (corner * other - off * off)
        left = (other * one - off * two) * inverse
        right = (corner * two - off * one) * inverse
        for group in range(at, size // 8):
            if group == at and inner == 6:
                continue
            first, second = firsts[group - at], seconds[group - at]
            if group == at:
                below = row_of > inner + 1
                first, second = jnp.where(below, first, 0.0), jnp.where(below, second, 0.0)
            groups[group] = groups[group] - (first * left + second * right)
        rows[pivot : pivot + 1, :] = (one * lax.rsqrt(corner))[0:1]
        ratio = off / corner
        rows[pivot + 1 : pivot + 2, :] = ((two - ratio * one) * lax.rsqrt(other - ratio * off))[0:1]
    upper = lax.broadcasted_iota(jnp.int32, (size, size), 0) <= lax.broadcasted_iota(
        jnp.int32, (size, size), 1
    )
    done = rows[...]
    factor_ref[...] = jnp.where(upper, done[:, :size], 0.0)
    basis_ref[...] = jnp.dot(
        done[:, size:],
        block_ref[...],
        precision=lax.Precision.HIGHEST,
        preferred_element_type=jnp.float32,
    )


def finish(gram, block):
    size = block.shape[0]
    return pl.pallas_call(
        finish_kernel,
        in_specs=[VMEM, VMEM],
        out_specs=[VMEM, VMEM],
        out_shape=[
            jax.ShapeDtypeStruct(block.shape, jnp.float32),
            jax.ShapeDtypeStruct((size, size), jnp.float32),
        ],
        scratch_shapes=[pltpu.VMEM((size, 2 * size), jnp.float32)],
        compiler_params=pltpu.CompilerParams(vmem_limit_bytes=LIMIT),
        name="factor_and_solve",
    )(gram, block)


def shards(start_block, operator_tiles, tile_pattern):
    vectors, node_count = start_block.shape
    rows_local, _, tile_size = operator_tiles.shape[:3]
    half = vectors // 2
    device_count = lax.axis_size(AXES)
    position = lax.axis_index(AXES)
    chip, core = position // 2, position % 2
    chip_rows = 2 * rows_local

    row_ids = jnp.arange(rows_local, dtype=jnp.int32)[:, None]
    away = tile_pattern - (position * rows_local + row_ids)
    start_tiles = start_block.reshape(vectors, rows_local, tile_size).transpose(1, 0, 2)
    low, high = start_tiles[:, :half], start_tiles[:, half:]
    slots = away.shape[1]
    packed = jnp.zeros((1, half, tile_size), jnp.bfloat16)
    packed = packed.at[0, :rows_local, :slots].set(away.astype(jnp.bfloat16))
    theirs = swapped(jnp.concatenate([jnp.where(core == 0, high, low), packed], axis=0))
    rounded = jnp.concatenate([jnp.where(core == 0, low, high), theirs[:rows_local]], axis=0)
    far_away = theirs[rows_local, :rows_local, :slots].astype(jnp.int32)

    tiles = turned(operator_tiles, swapped(operator_tiles))

    far_rows = (position ^ 1) * rows_local + row_ids
    columns = jnp.concatenate([tile_pattern, far_away + far_rows], axis=0)
    index = jnp.clip(columns - (chip - 1) * chip_rows, 0, 3 * chip_rows - 1)
    place, inner = index // chip_rows, (index % chip_rows) ^ (core * rows_local)
    index = jnp.where(chip % 2 == 1, (place + 1) % 3, place) * chip_rows + inner

    earlier = rounded.astype(jnp.float32)
    even_chip = (1 - chip % 2).reshape(1)
    latest, rounded = stepped(
        first_kernel,
        "first_step",
        (index, even_chip),
        (traded(rounded, 0), rounded, traded(rounded, 1), tiles),
    )
    for degree in range(2, DEG + 1):
        keep = (degree != DEG - 1, degree != DEG)
        made = stepped(
            functools.partial(step_kernel, keep),
            "step",
            (index,),
            (paired(rounded), traded(rounded, 1), tiles, earlier),
            keep,
        )
        earlier, latest, rounded = latest, made[0], made[-1]

    inner, outer = lax.axis_size("ry") // 2, lax.axis_size("rx")
    block, parts = gram_rows(
        core.reshape(1), latest, of_both_cores(latest), 1.0 / (node_count * device_count), inner
    )
    same_core = [list(range(low, 2 * inner, 2)) for low in (0, 1)]
    parts = lax.all_to_all(parts, "ry", 0, 0, axis_index_groups=same_core, tiled=True)
    parts = lax.all_to_all(summed(parts, outer), "rx", 0, 0, tiled=True)
    return tuple(finish(of_both_cores(summed(parts, 1)[0]), block))


def solution(mesh):
    return jax.shard_map(
        shards,
        mesh=mesh,
        in_specs=(P(None, AXES), P(AXES, None, None, None), P(AXES, None)),
        out_specs=(P(None, AXES), P()),
        check_vma=False,
    )
```

```python
import functools

import jax
import jax.numpy as jnp
from jax import lax
from jax.experimental import pallas as pl
from jax.experimental.pallas import tpu as pltpu
from jax.sharding import PartitionSpec as P

DEG = 12
AXES = ("rx", "ry")
VMEM = pl.BlockSpec(memory_space=pltpu.VMEM)
LIMIT = 16 * 2**20


def traded(value, first):
    count = lax.axis_size(AXES)
    route = []
    for low in range(2 * first, count - 2, 4):
        for core in (0, 1):
            route += [(low + core, low + core + 2), (low + core + 2, low + core)]
    return lax.ppermute(value, AXES, route)


def paired(value):
    groups = []
    for low in range(0, lax.axis_size("ry"), 4):
        groups += [[low, low + 2], [low + 1, low + 3]]
    return lax.all_gather(value, "ry", axis_index_groups=groups)


def of_both_cores(value):
    count = lax.axis_size("ry")
    groups = [[low, low + 1] for low in range(0, count, 2)]
    return lax.all_gather(value, "ry", axis_index_groups=groups)


def swapped(value):
    count = lax.axis_size(AXES)
    return lax.ppermute(value, AXES, [(source, source ^ 1) for source in range(count)])


def turn_kernel(near_ref, far_ref, out_ref):
    rows, slots = near_ref.shape[:2]
    for row in range(rows):
        for slot in range(slots):
            out_ref[row, slot] = near_ref[row, slot].T
            out_ref[rows + row, slot] = far_ref[row, slot].T


def turned(near, far):
    return pl.pallas_call(
        turn_kernel,
        in_specs=[VMEM, VMEM],
        out_specs=VMEM,
        out_shape=jax.ShapeDtypeStruct((2 * near.shape[0],) + near.shape[1:], near.dtype),
        compiler_params=pltpu.CompilerParams(vmem_limit_bytes=LIMIT),
        name="turn_tiles",
    )(near, far)


def apply_tiles(index_ref, tiles_ref, window, older_ref, latest_ref, rounded_ref):
    count, slots = tiles_ref.shape[:2]
    for row in range(count):
        total = None
        for slot in range(0, slots, 2):
            vectors = jnp.concatenate(
                [window[index_ref[row, slot]], window[index_ref[row, slot + 1]]], axis=1
            )
            tiles = jnp.concatenate([tiles_ref[row, slot], tiles_ref[row, slot + 1]], axis=0)
            part = jnp.dot(vectors, tiles, preferred_element_type=jnp.float32)
            total = part if total is None else total + part
        if older_ref is not None:
            total = 2.0 * total - older_ref[row]
        if latest_ref is not None:
            latest_ref[row] = total
        if rounded_ref is not None:
            rounded_ref[row] = total.astype(jnp.bfloat16)


def first_kernel(
    index_ref, even_chip_ref, even_ref, own_ref, odd_ref, tiles_ref, latest_ref, rounded_ref, window
):
    count = odd_ref.shape[0]
    is_even = even_chip_ref[0, 0] == 1
    own, even = own_ref[...], even_ref[...]
    window[0:count] = odd_ref[...]
    window[count : 2 * count] = jnp.where(is_even, own, even)
    window[2 * count : 3 * count] = jnp.where(is_even, even, own)
    apply_tiles(index_ref, tiles_ref, window, None, latest_ref, rounded_ref)


def step_kernel(keep, index_ref, pair_ref, odd_ref, tiles_ref, older_ref, *rest):
    latest_ref = rest[0] if keep[0] else None
    rounded_ref = rest[-2] if keep[1] else None
    window = rest[-1]
    count = odd_ref.shape[0]
    window[0:count] = odd_ref[...]
    window[count : 2 * count] = pair_ref[0]
    window[2 * count : 3 * count] = pair_ref[1]
    apply_tiles(index_ref, tiles_ref, window, older_ref, latest_ref, rounded_ref)


def stepped(kernel, name, scalars, blocks, keep=(True, True)):
    tiles = next(block for block in blocks if block.ndim == 4 and block.shape[-2] == block.shape[-1])
    shape = (tiles.shape[0], blocks[0].shape[-2], tiles.shape[2])
    kinds = [kind for kind, kept in zip((jnp.float32, jnp.bfloat16), keep) if kept]
    return pl.pallas_call(
        kernel,
        in_specs=[VMEM] * (len(scalars) + len(blocks)),
        out_specs=[VMEM] * len(kinds),
        out_shape=[jax.ShapeDtypeStruct(shape, kind) for kind in kinds],
        scratch_shapes=[pltpu.VMEM((3 * shape[0],) + shape[1:], jnp.bfloat16)],
        compiler_params=pltpu.CompilerParams(vmem_limit_bytes=LIMIT),
        cost_estimate=pl.CostEstimate(
            flops=2 * shape[1] * tiles.size, bytes_accessed=2 * tiles.size, transcendentals=0
        ),
        name=name,
    )(*scalars, *blocks)


def gram_kernel(scale, core_ref, mine_ref, both_ref, block_ref, part_ref, wide):
    tiles, half, width = mine_ref.shape
    core = core_ref[0, 0]
    even = core == 0
    for tile in range(tiles):
        mine, theirs = mine_ref[tile], both_ref[1 - core, (tile + tiles // 2) % tiles]
        columns = pl.ds(tile * width, width)
        wide[0:half, columns] = jnp.where(even, mine, theirs)
        wide[half : 2 * half, columns] = jnp.where(even, theirs, mine)
    block_ref[...] = wide[:, : tiles // 2 * width]
    mine = jnp.concatenate([mine_ref[tile] for tile in range(tiles)], axis=1)
    part = scale * lax.dot_general(
        mine,
        wide[...],
        (((1,), (1,)), ((), ())),
        precision=lax.Precision.HIGHEST,
        preferred_element_type=jnp.float32,
    )
    part = jnp.concatenate([part[: half // 2], part[half // 2 :]], axis=1)
    part_ref[...] = jnp.broadcast_to(part[None], part_ref.shape)


def gram_rows(core, mine, both, scale, copies):
    tiles, half, width = mine.shape
    return pl.pallas_call(
        functools.partial(gram_kernel, scale),
        in_specs=[VMEM, VMEM, VMEM],
        out_specs=[VMEM, VMEM],
        out_shape=[
            jax.ShapeDtypeStruct((2 * half, tiles // 2 * width), jnp.float32),
            jax.ShapeDtypeStruct((copies, half // 2, 4 * half), jnp.float32),
        ],
        scratch_shapes=[pltpu.VMEM((2 * half, tiles * width), jnp.float32)],
        compiler_params=pltpu.CompilerParams(vmem_limit_bytes=LIMIT),
        name="gram",
    )(core, mine, both)


def sum_kernel(parts_ref, out_ref):
    parts = [parts_ref[at] for at in range(parts_ref.shape[0])]
    while len(parts) > 1:
        parts = [one + other for one, other in zip(parts[::2], parts[1::2])]
    out_ref[...] = jnp.broadcast_to(parts[0][None], out_ref.shape)


def summed(parts, copies):
    return pl.pallas_call(
        sum_kernel,
        in_specs=[VMEM],
        out_specs=VMEM,
        out_shape=jax.ShapeDtypeStruct((copies,) + parts.shape[1:], parts.dtype),
        compiler_params=pltpu.CompilerParams(vmem_limit_bytes=LIMIT),
        name="sum_parts",
    )(parts)


def finish_kernel(gram_ref, block_ref, basis_ref, factor_ref, rows):
    size = block_ref.shape[0]
    quarter = size // 4
    lane_of = lax.broadcasted_iota(jnp.int32, (8, 2 * size), 1)
    row_of = lax.broadcasted_iota(jnp.int32, (8, 2 * size), 0)
    groups = []
    for group in range(size // 8):
        core, row = divmod(8 * group, 2 * quarter)
        part, row = divmod(row, quarter)
        stored = gram_ref[core, row : row + 8, part * size : (part + 1) * size]
        unit = (lane_of == row_of + (8 * group + size)).astype(jnp.float32)
        groups.append(jnp.concatenate([stored, unit[:, size:]], axis=1))
    def spread(value):
        return jnp.broadcast_to(value, (8, 2 * size))

    for pivot in range(0, size, 2):
        at, inner = divmod(pivot, 8)
        own = groups[at]
        one, two = spread(own[inner : inner + 1, :]), spread(own[inner + 1 : inner + 2, :])
        firsts = [spread(group[:, pivot : pivot + 1]) for group in groups[at:]]
        seconds = [spread(group[:, pivot + 1 : pivot + 2]) for group in groups[at:]]
        corner, off = spread(firsts[0][inner : inner + 1, :]), spread(seconds[0][inner : inner + 1, :])
        other = spread(seconds[0][inner + 1 : inner + 2, :])
        inverse = 1.0 / (corner * other - off * off)
        left = (other * one - off * two) * inverse
        right = (corner * two - off * one) * inverse
        for group in range(at, size // 8):
            if group == at and inner == 6:
                continue
            first, second = firsts[group - at], seconds[group - at]
            if group == at:
                below = row_of > inner + 1
                first, second = jnp.where(below, first, 0.0), jnp.where(below, second, 0.0)
            groups[group] = groups[group] - (first * left + second * right)
        rows[pivot : pivot + 1, :] = (one * lax.rsqrt(corner))[0:1]
        ratio = off / corner
        rows[pivot + 1 : pivot + 2, :] = ((two - ratio * one) * lax.rsqrt(other - ratio * off))[0:1]
    upper = lax.broadcasted_iota(jnp.int32, (size, size), 0) <= lax.broadcasted_iota(
        jnp.int32, (size, size), 1
    )
    done = rows[...]
    factor_ref[...] = jnp.where(upper, done[:, :size], 0.0)
    basis_ref[...] = jnp.dot(
        done[:, size:],
        block_ref[...],
        precision=lax.Precision.HIGHEST,
        preferred_element_type=jnp.float32,
    )


def finish(gram, block):
    size = block.shape[0]
    return pl.pallas_call(
        finish_kernel,
        in_specs=[VMEM, VMEM],
        out_specs=[VMEM, VMEM],
        out_shape=[
            jax.ShapeDtypeStruct(block.shape, jnp.float32),
            jax.ShapeDtypeStruct((size, size), jnp.float32),
        ],
        scratch_shapes=[pltpu.VMEM((size, 2 * size), jnp.float32)],
        compiler_params=pltpu.CompilerParams(vmem_limit_bytes=LIMIT),
        name="factor_and_solve",
    )(gram, block)


def shards(start_block, operator_tiles, tile_pattern):
    vectors, node_count = start_block.shape
    rows_local, _, tile_size = operator_tiles.shape[:3]
    half = vectors // 2
    device_count = lax.axis_size(AXES)
    position = lax.axis_index(AXES)
    chip, core = position // 2, position % 2
    chip_rows = 2 * rows_local

    row_ids = jnp.arange(rows_local, dtype=jnp.int32)[:, None]
    away = tile_pattern - (position * rows_local + row_ids)
    start_tiles = start_block.reshape(vectors, rows_local, tile_size).transpose(1, 0, 2)
    low, high = start_tiles[:, :half], start_tiles[:, half:]
    slots = away.shape[1]
    packed = jnp.zeros((1, half, tile_size), jnp.bfloat16)
    packed = packed.at[0, :rows_local, :slots].set(away.astype(jnp.bfloat16))
    theirs = swapped(jnp.concatenate([jnp.where(core == 0, high, low), packed], axis=0))
    rounded = jnp.concatenate([jnp.where(core == 0, low, high), theirs[:rows_local]], axis=0)
    far_away = theirs[rows_local, :rows_local, :slots].astype(jnp.int32)

    tiles = turned(operator_tiles, swapped(operator_tiles))

    far_rows = (position ^ 1) * rows_local + row_ids
    columns = jnp.concatenate([tile_pattern, far_away + far_rows], axis=0)
    index = jnp.clip(columns - (chip - 1) * chip_rows, 0, 3 * chip_rows - 1)
    place, inner = index // chip_rows, (index % chip_rows) ^ (core * rows_local)
    index = jnp.where(chip % 2 == 1, (place + 1) % 3, place) * chip_rows + inner

    earlier = rounded.astype(jnp.float32)
    even_chip = (1 - chip % 2).reshape(1, 1)
    latest, rounded = stepped(
        first_kernel,
        "first_step",
        (index, even_chip),
        (traded(rounded, 0), rounded, traded(rounded, 1), tiles),
    )
    for degree in range(2, DEG + 1):
        keep = (degree != DEG - 1, degree != DEG)
        made = stepped(
            functools.partial(step_kernel, keep),
            "step",
            (index,),
            (paired(rounded), traded(rounded, 1), tiles, earlier),
            keep,
        )
        earlier, latest, rounded = latest, made[0], made[-1]

    inner, outer = lax.axis_size("ry") // 2, lax.axis_size("rx")
    block, parts = gram_rows(
        core.reshape(1, 1), latest, of_both_cores(latest), 1.0 / (node_count * device_count), inner
    )
    same_core = [list(range(low, 2 * inner, 2)) for low in (0, 1)]
    parts = lax.all_to_all(parts, "ry", 0, 0, axis_index_groups=same_core, tiled=True)
    parts = lax.all_to_all(summed(parts, outer), "rx", 0, 0, tiled=True)
    return tuple(finish(of_both_cores(summed(parts, 1)[0]), block))


def solution(mesh):
    return jax.shard_map(
        shards,
        mesh=mesh,
        in_specs=(P(None, AXES), P(AXES, None, None, None), P(AXES, None)),
        out_specs=(P(None, AXES), P()),
        check_vma=False,
    )
```

```python
import functools

import jax
import jax.numpy as jnp
from jax import lax
from jax.experimental import pallas as pl
from jax.experimental.pallas import tpu as pltpu
from jax.sharding import PartitionSpec as P

DEG = 12
AXES = ("rx", "ry")
VMEM = pl.BlockSpec(memory_space=pltpu.VMEM)
LIMIT = 16 * 2**20


def traded(value, first):
    count = lax.axis_size(AXES)
    route = []
    for low in range(2 * first, count - 2, 4):
        for core in (0, 1):
            route += [(low + core, low + core + 2), (low + core + 2, low + core)]
    return lax.ppermute(value, AXES, route)


def paired(value):
    groups = []
    for low in range(0, lax.axis_size("ry"), 4):
        groups += [[low, low + 2], [low + 1, low + 3]]
    return lax.all_gather(value, "ry", axis_index_groups=groups)


def of_both_cores(value):
    count = lax.axis_size("ry")
    groups = [[low, low + 1] for low in range(0, count, 2)]
    return lax.all_gather(value, "ry", axis_index_groups=groups)


def swapped(value):
    count = lax.axis_size(AXES)
    return lax.ppermute(value, AXES, [(source, source ^ 1) for source in range(count)])


def turn_kernel(near_ref, far_ref, out_ref):
    rows, slots = near_ref.shape[:2]
    for row in range(rows):
        for slot in range(slots):
            out_ref[row, slot] = near_ref[row, slot].T
            out_ref[rows + row, slot] = far_ref[row, slot].T


def turned(near, far):
    return pl.pallas_call(
        turn_kernel,
        in_specs=[VMEM, VMEM],
        out_specs=VMEM,
        out_shape=jax.ShapeDtypeStruct((2 * near.shape[0],) + near.shape[1:], near.dtype),
        compiler_params=pltpu.CompilerParams(vmem_limit_bytes=LIMIT),
        name="turn_tiles",
    )(near, far)


def apply_tiles(index_ref, tiles_ref, window, older_ref, latest_ref, rounded_ref):
    count, slots = tiles_ref.shape[:2]
    for row in range(count):
        total = None
        for slot in range(0, slots, 2):
            vectors = jnp.concatenate(
                [window[index_ref[row, slot]], window[index_ref[row, slot + 1]]], axis=1
            )
            tiles = jnp.concatenate([tiles_ref[row, slot], tiles_ref[row, slot + 1]], axis=0)
            part = jnp.dot(vectors, tiles, preferred_element_type=jnp.float32)
            total = part if total is None else total + part
        if older_ref is not None:
            total = 2.0 * total - older_ref[row]
        if latest_ref is not None:
            latest_ref[row] = total
        if rounded_ref is not None:
            rounded_ref[row] = total.astype(jnp.bfloat16)


def first_kernel(
    index_ref, even_chip_ref, even_ref, own_ref, odd_ref, tiles_ref, latest_ref, rounded_ref, window
):
    count = odd_ref.shape[0]
    is_even = even_chip_ref[0, 0] == 1
    own, even = own_ref[...], even_ref[...]
    window[0:count] = odd_ref[...]
    window[count : 2 * count] = jnp.where(is_even, own, even)
    window[2 * count : 3 * count] = jnp.where(is_even, even, own)
    apply_tiles(index_ref, tiles_ref, window, None, latest_ref, rounded_ref)


def step_kernel(keep, index_ref, pair_ref, odd_ref, tiles_ref, older_ref, *rest):
    latest_ref = rest[0] if keep[0] else None
    rounded_ref = rest[-2] if keep[1] else None
    window = rest[-1]
    count = odd_ref.shape[0]
    window[0:count] = odd_ref[...]
    window[count : 2 * count] = pair_ref[0]
    window[2 * count : 3 * count] = pair_ref[1]
    apply_tiles(index_ref, tiles_ref, window, older_ref, latest_ref, rounded_ref)


def stepped(kernel, name, scalars, blocks, keep=(True, True)):
    tiles = next(block for block in blocks if block.ndim == 4 and block.shape[-2] == block.shape[-1])
    shape = (tiles.shape[0], blocks[0].shape[-2], tiles.shape[2])
    kinds = [kind for kind, kept in zip((jnp.float32, jnp.bfloat16), keep) if kept]
    return pl.pallas_call(
        kernel,
        in_specs=[VMEM] * (len(scalars) + len(blocks)),
        out_specs=[VMEM] * len(kinds),
        out_shape=[jax.ShapeDtypeStruct(shape, kind) for kind in kinds],
        scratch_shapes=[pltpu.VMEM((3 * shape[0],) + shape[1:], jnp.bfloat16)],
        compiler_params=pltpu.CompilerParams(vmem_limit_bytes=LIMIT),
        cost_estimate=pl.CostEstimate(
            flops=2 * shape[1] * tiles.size, bytes_accessed=2 * tiles.size, transcendentals=0
        ),
        name=name,
    )(*scalars, *blocks)


def gram_kernel(scale, core_ref, mine_ref, both_ref, block_ref, part_ref, wide):
    tiles, half, width = mine_ref.shape
    core = core_ref[0, 0]
    even = core == 0
    for tile in range(tiles):
        mine, theirs = mine_ref[tile], both_ref[1 - core, (tile + tiles // 2) % tiles]
        columns = pl.ds(tile * width, width)
        wide[0:half, columns] = jnp.where(even, mine, theirs)
        wide[half : 2 * half, columns] = jnp.where(even, theirs, mine)
    block_ref[...] = wide[:, : tiles // 2 * width]
    mine = jnp.concatenate([mine_ref[tile] for tile in range(tiles)], axis=1)
    part = scale * lax.dot_general(
        mine,
        wide[...],
        (((1,), (1,)), ((), ())),
        precision=lax.Precision.HIGHEST,
        preferred_element_type=jnp.float32,
    )
    part = jnp.concatenate([part[: half // 2], part[half // 2 :]], axis=1)
    part_ref[...] = jnp.broadcast_to(part[None], part_ref.shape)


def gram_rows(core, mine, both, scale, copies):
    tiles, half, width = mine.shape
    return pl.pallas_call(
        functools.partial(gram_kernel, scale),
        in_specs=[VMEM, VMEM, VMEM],
        out_specs=[VMEM, VMEM],
        out_shape=[
            jax.ShapeDtypeStruct((2 * half, tiles // 2 * width), jnp.float32),
            jax.ShapeDtypeStruct((copies, half // 2, 4 * half), jnp.float32),
        ],
        scratch_shapes=[pltpu.VMEM((2 * half, tiles * width), jnp.float32)],
        compiler_params=pltpu.CompilerParams(vmem_limit_bytes=LIMIT),
        name="gram",
    )(core, mine, both)


def sum_kernel(parts_ref, out_ref):
    parts = [parts_ref[at] for at in range(parts_ref.shape[0])]
    while len(parts) > 1:
        parts = [one + other for one, other in zip(parts[::2], parts[1::2])]
    out_ref[...] = jnp.broadcast_to(parts[0][None], out_ref.shape)


def summed(parts, copies):
    return pl.pallas_call(
        sum_kernel,
        in_specs=[VMEM],
        out_specs=VMEM,
        out_shape=jax.ShapeDtypeStruct((copies,) + parts.shape[1:], parts.dtype),
        compiler_params=pltpu.CompilerParams(vmem_limit_bytes=LIMIT),
        name="sum_parts",
    )(parts)


def finish_kernel(gram_ref, block_ref, basis_ref, factor_ref, rows):
    size = block_ref.shape[0]
    quarter = size // 4
    lane_of = lax.broadcasted_iota(jnp.int32, (8, 2 * size), 1)
    row_of = lax.broadcasted_iota(jnp.int32, (8, 2 * size), 0)
    groups = []
    for group in range(size // 8):
        core, row = divmod(8 * group, 2 * quarter)
        part, row = divmod(row, quarter)
        stored = gram_ref[core, row : row + 8, part * size : (part + 1) * size]
        unit = (lane_of == row_of + (8 * group + size)).astype(jnp.float32)
        groups.append(jnp.concatenate([stored, unit[:, size:]], axis=1))
    def spread(value):
        return jnp.broadcast_to(value, (8, 2 * size))

    for pivot in range(0, size, 4):
        at, inner = divmod(pivot, 8)
        columns = [
            [spread(group[:, pivot + i : pivot + i + 1]) for i in range(4)] for group in groups[at:]
        ]
        lines = [spread(groups[at][inner + i : inner + i + 1, :]) for i in range(4)]
        block = [
            [spread(columns[0][j][inner + i : inner + i + 1, :]) for j in range(i + 1)] for i in range(4)
        ]
        inverses, scales = [], []
        lower = [[None] * 4 for _ in range(4)]
        for j in range(4):
            inverse = 1.0 / block[j][j]
            inverses.append(inverse)
            scales.append(lax.rsqrt(block[j][j]))
            for i in range(j + 1, 4):
                lower[i][j] = block[i][j] * inverse
            for i in range(j + 1, 4):
                for k in range(j + 1, i + 1):
                    block[i][k] = block[i][k] - lower[i][j] * block[k][j]
        for j in range(4):
            for i in range(j + 1, 4):
                lines[i] = lines[i] - lower[i][j] * lines[j]
            rows[pivot + j : pivot + j + 1, :] = (lines[j] * scales[j])[0:1]
        for group in range(at, size // 8):
            if group == at and inner == 4:
                continue
            own = columns[group - at]
            change = None
            for j in range(4):
                for i in range(j + 1, 4):
                    own[i] = own[i] - lower[i][j] * own[j]
                part = own[j] * inverses[j] * lines[j]
                change = part if change is None else change + part
            if group == at:
                change = jnp.where(row_of > inner + 3, change, 0.0)
            groups[group] = groups[group] - change
    upper = lax.broadcasted_iota(jnp.int32, (size, size), 0) <= lax.broadcasted_iota(
        jnp.int32, (size, size), 1
    )
    done = rows[...]
    factor_ref[...] = jnp.where(upper, done[:, :size], 0.0)
    basis_ref[...] = jnp.dot(
        done[:, size:],
        block_ref[...],
        precision=lax.Precision.HIGHEST,
        preferred_element_type=jnp.float32,
    )


def finish(gram, block):
    size = block.shape[0]
    return pl.pallas_call(
        finish_kernel,
        in_specs=[VMEM, VMEM],
        out_specs=[VMEM, VMEM],
        out_shape=[
            jax.ShapeDtypeStruct(block.shape, jnp.float32),
            jax.ShapeDtypeStruct((size, size), jnp.float32),
        ],
        scratch_shapes=[pltpu.VMEM((size, 2 * size), jnp.float32)],
        compiler_params=pltpu.CompilerParams(vmem_limit_bytes=LIMIT),
        name="factor_and_solve",
    )(gram, block)


def shards(start_block, operator_tiles, tile_pattern):
    vectors, node_count = start_block.shape
    rows_local, _, tile_size = operator_tiles.shape[:3]
    half = vectors // 2
    device_count = lax.axis_size(AXES)
    position = lax.axis_index(AXES)
    chip, core = position // 2, position % 2
    chip_rows = 2 * rows_local

    row_ids = jnp.arange(rows_local, dtype=jnp.int32)[:, None]
    away = tile_pattern - (position * rows_local + row_ids)
    start_tiles = start_block.reshape(vectors, rows_local, tile_size).transpose(1, 0, 2)
    low, high = start_tiles[:, :half], start_tiles[:, half:]
    slots = away.shape[1]
    packed = jnp.zeros((1, half, tile_size), jnp.bfloat16)
    packed = packed.at[0, :rows_local, :slots].set(away.astype(jnp.bfloat16))
    sent = of_both_cores(jnp.concatenate([jnp.where(core == 0, high, low), packed], axis=0))
    theirs = jnp.where(core == 0, sent[1], sent[0])
    rounded = jnp.concatenate([jnp.where(core == 0, low, high), theirs[:rows_local]], axis=0)
    far_away = theirs[rows_local, :rows_local, :slots].astype(jnp.int32)

    tiles = turned(operator_tiles, swapped(operator_tiles))

    far_rows = (position ^ 1) * rows_local + row_ids
    columns = jnp.concatenate([tile_pattern, far_away + far_rows], axis=0)
    index = jnp.clip(columns - (chip - 1) * chip_rows, 0, 3 * chip_rows - 1)
    place, inner = index // chip_rows, (index % chip_rows) ^ (core * rows_local)
    index = jnp.where(chip % 2 == 1, (place + 1) % 3, place) * chip_rows + inner

    earlier = rounded.astype(jnp.float32)
    even_chip = (1 - chip % 2).reshape(1, 1)
    latest, rounded = stepped(
        first_kernel,
        "first_step",
        (index, even_chip),
        (traded(rounded, 0), rounded, traded(rounded, 1), tiles),
    )
    for degree in range(2, DEG + 1):
        keep = (degree != DEG - 1, degree != DEG)
        made = stepped(
            functools.partial(step_kernel, keep),
            "step",
            (index,),
            (paired(rounded), traded(rounded, 1), tiles, earlier),
            keep,
        )
        earlier, latest, rounded = latest, made[0], made[-1]

    inner, outer = lax.axis_size("ry") // 2, lax.axis_size("rx")
    block, parts = gram_rows(
        core.reshape(1, 1), latest, of_both_cores(latest), 1.0 / (node_count * device_count), inner
    )
    same_core = [list(range(low, 2 * inner, 2)) for low in (0, 1)]
    parts = lax.all_to_all(parts, "ry", 0, 0, axis_index_groups=same_core, tiled=True)
    parts = lax.all_to_all(summed(parts, outer), "rx", 0, 0, tiled=True)
    return tuple(finish(of_both_cores(summed(parts, 1)[0]), block))


def solution(mesh):
    return jax.shard_map(
        shards,
        mesh=mesh,
        in_specs=(P(None, AXES), P(AXES, None, None, None), P(AXES, None)),
        out_specs=(P(None, AXES), P()),
        check_vma=False,
    )
```

```python
import functools

import jax
import jax.numpy as jnp
from jax import lax
from jax.experimental import pallas as pl
from jax.experimental.pallas import tpu as pltpu
from jax.sharding import PartitionSpec as P

DEG = 12
AXES = ("rx", "ry")
VMEM = pl.BlockSpec(memory_space=pltpu.VMEM)
LIMIT = 16 * 2**20


def traded(value, first):
    count = lax.axis_size(AXES)
    route = []
    for low in range(2 * first, count - 2, 4):
        for core in (0, 1):
            route += [(low + core, low + core + 2), (low + core + 2, low + core)]
    return lax.ppermute(value, AXES, route)


def paired(value):
    groups = []
    for low in range(0, lax.axis_size("ry"), 4):
        groups += [[low, low + 2], [low + 1, low + 3]]
    return lax.all_gather(value, "ry", axis_index_groups=groups)


def of_both_cores(value):
    count = lax.axis_size("ry")
    groups = [[low, low + 1] for low in range(0, count, 2)]
    return lax.all_gather(value, "ry", axis_index_groups=groups)


def swapped(value):
    count = lax.axis_size(AXES)
    return lax.ppermute(value, AXES, [(source, source ^ 1) for source in range(count)])


def turn_kernel(near_ref, far_ref, out_ref):
    rows, slots = near_ref.shape[:2]
    for row in range(rows):
        for slot in range(slots):
            out_ref[row, slot] = near_ref[row, slot].T
            out_ref[rows + row, slot] = far_ref[row, slot].T


def turned(near, far):
    return pl.pallas_call(
        turn_kernel,
        in_specs=[VMEM, VMEM],
        out_specs=VMEM,
        out_shape=jax.ShapeDtypeStruct((2 * near.shape[0],) + near.shape[1:], near.dtype),
        compiler_params=pltpu.CompilerParams(vmem_limit_bytes=LIMIT),
        name="turn_tiles",
    )(near, far)


def apply_tiles(index_ref, tiles_ref, window, older_ref, latest_ref, rounded_ref):
    count, slots = tiles_ref.shape[:2]
    for row in range(count):
        total = None
        for slot in range(0, slots, 2):
            vectors = jnp.concatenate(
                [window[index_ref[row, slot]], window[index_ref[row, slot + 1]]], axis=1
            )
            tiles = jnp.concatenate([tiles_ref[row, slot], tiles_ref[row, slot + 1]], axis=0)
            part = jnp.dot(vectors, tiles, preferred_element_type=jnp.float32)
            total = part if total is None else total + part
        if older_ref is not None:
            total = 2.0 * total - older_ref[row]
        if latest_ref is not None:
            latest_ref[row] = total
        if rounded_ref is not None:
            rounded_ref[row] = total.astype(jnp.bfloat16)


def first_kernel(
    index_ref, even_chip_ref, odd_ref, own_ref, even_ref, tiles_ref, latest_ref, rounded_ref, window
):
    count = odd_ref.shape[0]
    is_even = even_chip_ref[0, 0] == 1
    own, even = own_ref[...], even_ref[...]
    window[0:count] = odd_ref[...]
    window[count : 2 * count] = jnp.where(is_even, own, even)
    window[2 * count : 3 * count] = jnp.where(is_even, even, own)
    apply_tiles(index_ref, tiles_ref, window, None, latest_ref, rounded_ref)


def step_kernel(keep, index_ref, pair_ref, odd_ref, tiles_ref, older_ref, *rest):
    latest_ref = rest[0] if keep[0] else None
    rounded_ref = rest[-2] if keep[1] else None
    window = rest[-1]
    count = odd_ref.shape[0]
    window[0:count] = odd_ref[...]
    window[count : 2 * count] = pair_ref[0]
    window[2 * count : 3 * count] = pair_ref[1]
    apply_tiles(index_ref, tiles_ref, window, older_ref, latest_ref, rounded_ref)


def stepped(kernel, name, scalars, blocks, keep=(True, True)):
    tiles = next(block for block in blocks if block.ndim == 4 and block.shape[-2] == block.shape[-1])
    shape = (tiles.shape[0], blocks[0].shape[-2], tiles.shape[2])
    kinds = [kind for kind, kept in zip((jnp.float32, jnp.bfloat16), keep) if kept]
    return pl.pallas_call(
        kernel,
        in_specs=[VMEM] * (len(scalars) + len(blocks)),
        out_specs=[VMEM] * len(kinds),
        out_shape=[jax.ShapeDtypeStruct(shape, kind) for kind in kinds],
        scratch_shapes=[pltpu.VMEM((3 * shape[0],) + shape[1:], jnp.bfloat16)],
        compiler_params=pltpu.CompilerParams(vmem_limit_bytes=LIMIT),
        cost_estimate=pl.CostEstimate(
            flops=2 * shape[1] * tiles.size, bytes_accessed=2 * tiles.size, transcendentals=0
        ),
        name=name,
    )(*scalars, *blocks)


def gram_kernel(scale, core_ref, mine_ref, both_ref, block_ref, part_ref, wide):
    tiles, half, width = mine_ref.shape
    core = core_ref[0, 0]
    even = core == 0
    for tile in range(tiles):
        mine, theirs = mine_ref[tile], both_ref[1 - core, (tile + tiles // 2) % tiles]
        columns = pl.ds(tile * width, width)
        wide[0:half, columns] = jnp.where(even, mine, theirs)
        wide[half : 2 * half, columns] = jnp.where(even, theirs, mine)
    block_ref[...] = wide[:, : tiles // 2 * width]
    mine = jnp.concatenate([mine_ref[tile] for tile in range(tiles)], axis=1)
    part = scale * lax.dot_general(
        mine,
        wide[...],
        (((1,), (1,)), ((), ())),
        precision=lax.Precision.HIGHEST,
        preferred_element_type=jnp.float32,
    )
    part = jnp.concatenate([part[: half // 2], part[half // 2 :]], axis=1)
    part_ref[...] = jnp.broadcast_to(part[None], part_ref.shape)


def gram_rows(core, mine, both, scale, copies):
    tiles, half, width = mine.shape
    return pl.pallas_call(
        functools.partial(gram_kernel, scale),
        in_specs=[VMEM, VMEM, VMEM],
        out_specs=[VMEM, VMEM],
        out_shape=[
            jax.ShapeDtypeStruct((2 * half, tiles // 2 * width), jnp.float32),
            jax.ShapeDtypeStruct((copies, half // 2, 4 * half), jnp.float32),
        ],
        scratch_shapes=[pltpu.VMEM((2 * half, tiles * width), jnp.float32)],
        compiler_params=pltpu.CompilerParams(vmem_limit_bytes=LIMIT),
        name="gram",
    )(core, mine, both)


def sum_kernel(parts_ref, out_ref):
    parts = [parts_ref[at] for at in range(parts_ref.shape[0])]
    while len(parts) > 1:
        parts = [one + other for one, other in zip(parts[::2], parts[1::2])]
    out_ref[...] = jnp.broadcast_to(parts[0][None], out_ref.shape)


def summed(parts, copies):
    return pl.pallas_call(
        sum_kernel,
        in_specs=[VMEM],
        out_specs=VMEM,
        out_shape=jax.ShapeDtypeStruct((copies,) + parts.shape[1:], parts.dtype),
        compiler_params=pltpu.CompilerParams(vmem_limit_bytes=LIMIT),
        name="sum_parts",
    )(parts)


def finish_kernel(gram_ref, block_ref, basis_ref, factor_ref, rows):
    size = block_ref.shape[0]
    quarter = size // 4
    lane_of = lax.broadcasted_iota(jnp.int32, (8, 2 * size), 1)
    row_of = lax.broadcasted_iota(jnp.int32, (8, 2 * size), 0)
    groups = []
    for group in range(size // 8):
        core, row = divmod(8 * group, 2 * quarter)
        part, row = divmod(row, quarter)
        stored = gram_ref[core, row : row + 8, part * size : (part + 1) * size]
        unit = (lane_of == row_of + (8 * group + size)).astype(jnp.float32)
        groups.append(jnp.concatenate([stored, unit[:, size:]], axis=1))
    def spread(value):
        return jnp.broadcast_to(value, (8, 2 * size))

    for pivot in range(0, size, 4):
        at, inner = divmod(pivot, 8)
        columns = [
            [spread(group[:, pivot + i : pivot + i + 1]) for i in range(4)] for group in groups[at:]
        ]
        lines = [spread(groups[at][inner + i : inner + i + 1, :]) for i in range(4)]
        block = [
            [spread(columns[0][j][inner + i : inner + i + 1, :]) for j in range(i + 1)] for i in range(4)
        ]
        inverses, scales = [], []
        lower = [[None] * 4 for _ in range(4)]
        for j in range(4):
            inverse = 1.0 / block[j][j]
            inverses.append(inverse)
            scales.append(lax.rsqrt(block[j][j]))
            for i in range(j + 1, 4):
                lower[i][j] = block[i][j] * inverse
            for i in range(j + 1, 4):
                for k in range(j + 1, i + 1):
                    block[i][k] = block[i][k] - lower[i][j] * block[k][j]
        for j in range(4):
            for i in range(j + 1, 4):
                lines[i] = lines[i] - lower[i][j] * lines[j]
            rows[pivot + j : pivot + j + 1, :] = (lines[j] * scales[j])[0:1]
        for group in range(at, size // 8):
            if group == at and inner == 4:
                continue
            own = columns[group - at]
            change = None
            for j in range(4):
                for i in range(j + 1, 4):
                    own[i] = own[i] - lower[i][j] * own[j]
                part = own[j] * inverses[j] * lines[j]
                change = part if change is None else change + part
            if group == at:
                change = jnp.where(row_of > inner + 3, change, 0.0)
            groups[group] = groups[group] - change
    upper = lax.broadcasted_iota(jnp.int32, (size, size), 0) <= lax.broadcasted_iota(
        jnp.int32, (size, size), 1
    )
    done = rows[...]
    factor_ref[...] = jnp.where(upper, done[:, :size], 0.0)
    basis_ref[...] = jnp.dot(
        done[:, size:],
        block_ref[...],
        precision=lax.Precision.HIGHEST,
        preferred_element_type=jnp.float32,
    )


def finish(gram, block):
    size = block.shape[0]
    return pl.pallas_call(
        finish_kernel,
        in_specs=[VMEM, VMEM],
        out_specs=[VMEM, VMEM],
        out_shape=[
            jax.ShapeDtypeStruct(block.shape, jnp.float32),
            jax.ShapeDtypeStruct((size, size), jnp.float32),
        ],
        scratch_shapes=[pltpu.VMEM((size, 2 * size), jnp.float32)],
        compiler_params=pltpu.CompilerParams(vmem_limit_bytes=LIMIT),
        name="factor_and_solve",
    )(gram, block)


def shards(start_block, operator_tiles, tile_pattern):
    vectors, node_count = start_block.shape
    rows_local, _, tile_size = operator_tiles.shape[:3]
    half = vectors // 2
    device_count = lax.axis_size(AXES)
    position = lax.axis_index(AXES)
    chip, core = position // 2, position % 2
    chip_rows = 2 * rows_local

    row_ids = jnp.arange(rows_local, dtype=jnp.int32)[:, None]
    away = tile_pattern - (position * rows_local + row_ids)
    start_tiles = start_block.reshape(vectors, rows_local, tile_size).transpose(1, 0, 2)
    low, high = start_tiles[:, :half], start_tiles[:, half:]
    slots = away.shape[1]
    packed = jnp.zeros((1, half, tile_size), jnp.bfloat16)
    packed = packed.at[0, :rows_local, :slots].set(away.astype(jnp.bfloat16))
    sent = of_both_cores(jnp.concatenate([jnp.where(core == 0, high, low), packed], axis=0))
    theirs = jnp.where(core == 0, sent[1], sent[0])
    rounded = jnp.concatenate([jnp.where(core == 0, low, high), theirs[:rows_local]], axis=0)
    far_away = theirs[rows_local, :rows_local, :slots].astype(jnp.int32)

    operator_tiles, rounded = lax.optimization_barrier((operator_tiles, rounded))
    tiles = turned(operator_tiles, swapped(operator_tiles))

    far_rows = (position ^ 1) * rows_local + row_ids
    columns = jnp.concatenate([tile_pattern, far_away + far_rows], axis=0)
    index = jnp.clip(columns - (chip - 1) * chip_rows, 0, 3 * chip_rows - 1)
    place, inner = index // chip_rows, (index % chip_rows) ^ (core * rows_local)
    index = jnp.where(chip % 2 == 1, (place + 1) % 3, place) * chip_rows + inner

    earlier = rounded.astype(jnp.float32)
    even_chip = (1 - chip % 2).reshape(1, 1)
    latest, rounded = stepped(
        first_kernel,
        "first_step",
        (index, even_chip),
        (traded(rounded, 1), rounded, traded(rounded, 0), tiles),
    )
    for degree in range(2, DEG + 1):
        keep = (degree != DEG - 1, degree != DEG)
        made = stepped(
            functools.partial(step_kernel, keep),
            "step",
            (index,),
            (paired(rounded), traded(rounded, 1), tiles, earlier),
            keep,
        )
        earlier, latest, rounded = latest, made[0], made[-1]

    inner, outer = lax.axis_size("ry") // 2, lax.axis_size("rx")
    block, parts = gram_rows(
        core.reshape(1, 1), latest, of_both_cores(latest), 1.0 / (node_count * device_count), inner
    )
    same_core = [list(range(low, 2 * inner, 2)) for low in (0, 1)]
    parts = lax.all_to_all(parts, "ry", 0, 0, axis_index_groups=same_core, tiled=True)
    parts = lax.all_to_all(summed(parts, outer), "rx", 0, 0, tiled=True)
    return tuple(finish(of_both_cores(summed(parts, 1)[0]), block))


def solution(mesh):
    return jax.shard_map(
        shards,
        mesh=mesh,
        in_specs=(P(None, AXES), P(AXES, None, None, None), P(AXES, None)),
        out_specs=(P(None, AXES), P()),
        check_vma=False,
    )
```

```python
import functools

import jax
import jax.numpy as jnp
from jax import lax
from jax.experimental import pallas as pl
from jax.experimental.pallas import tpu as pltpu
from jax.sharding import PartitionSpec as P

DEG = 12
AXES = ("rx", "ry")
VMEM = pl.BlockSpec(memory_space=pltpu.VMEM)
LIMIT = 16 * 2**20


def traded(value, first):
    count = lax.axis_size(AXES)
    route = []
    for low in range(2 * first, count - 2, 4):
        for core in (0, 1):
            route += [(low + core, low + core + 2), (low + core + 2, low + core)]
    return lax.ppermute(value, AXES, route)


def paired(value):
    groups = []
    for low in range(0, lax.axis_size("ry"), 4):
        groups += [[low, low + 2], [low + 1, low + 3]]
    return lax.all_gather(value, "ry", axis_index_groups=groups)


def of_both_cores(value):
    count = lax.axis_size("ry")
    groups = [[low, low + 1] for low in range(0, count, 2)]
    return lax.all_gather(value, "ry", axis_index_groups=groups)


def swapped(value):
    count = lax.axis_size(AXES)
    return lax.ppermute(value, AXES, [(source, source ^ 1) for source in range(count)])


def turn_kernel(near_ref, far_ref, out_ref):
    rows, slots = near_ref.shape[:2]
    for row in range(rows):
        for slot in range(slots):
            out_ref[row, slot] = near_ref[row, slot].T
            out_ref[rows + row, slot] = far_ref[row, slot].T


def turned(near, far):
    return pl.pallas_call(
        turn_kernel,
        in_specs=[VMEM, VMEM],
        out_specs=VMEM,
        out_shape=jax.ShapeDtypeStruct((2 * near.shape[0],) + near.shape[1:], near.dtype),
        compiler_params=pltpu.CompilerParams(vmem_limit_bytes=LIMIT),
        name="turn_tiles",
    )(near, far)


def apply_tiles(index_ref, tiles_ref, window, older_ref, latest_ref, rounded_ref):
    count, slots = tiles_ref.shape[:2]
    for row in range(count):
        total = None
        for slot in range(0, slots, 2):
            vectors = jnp.concatenate(
                [window[index_ref[row, slot]], window[index_ref[row, slot + 1]]], axis=1
            )
            tiles = jnp.concatenate([tiles_ref[row, slot], tiles_ref[row, slot + 1]], axis=0)
            part = jnp.dot(vectors, tiles, preferred_element_type=jnp.float32)
            total = part if total is None else total + part
        if older_ref is not None:
            total = 2.0 * total - older_ref[row]
        if latest_ref is not None:
            latest_ref[row] = total
        if rounded_ref is not None:
            rounded_ref[row] = total.astype(jnp.bfloat16)


def first_kernel(
    index_ref, even_chip_ref, odd_ref, own_ref, even_ref, tiles_ref, latest_ref, rounded_ref, window
):
    count = odd_ref.shape[0]
    is_even = even_chip_ref[0, 0] == 1
    own, even = own_ref[...], even_ref[...]
    window[0:count] = odd_ref[...]
    window[count : 2 * count] = jnp.where(is_even, own, even)
    window[2 * count : 3 * count] = jnp.where(is_even, even, own)
    apply_tiles(index_ref, tiles_ref, window, None, latest_ref, rounded_ref)


def step_kernel(keep, index_ref, pair_ref, odd_ref, tiles_ref, older_ref, *rest):
    latest_ref = rest[0] if keep[0] else None
    rounded_ref = rest[-2] if keep[1] else None
    window = rest[-1]
    count = odd_ref.shape[0]
    window[0:count] = odd_ref[...]
    window[count : 2 * count] = pair_ref[0]
    window[2 * count : 3 * count] = pair_ref[1]
    apply_tiles(index_ref, tiles_ref, window, older_ref, latest_ref, rounded_ref)


def stepped(kernel, name, scalars, blocks, keep=(True, True)):
    tiles = next(block for block in blocks if block.ndim == 4 and block.shape[-2] == block.shape[-1])
    shape = (tiles.shape[0], blocks[0].shape[-2], tiles.shape[2])
    kinds = [kind for kind, kept in zip((jnp.float32, jnp.bfloat16), keep) if kept]
    return pl.pallas_call(
        kernel,
        in_specs=[VMEM] * (len(scalars) + len(blocks)),
        out_specs=[VMEM] * len(kinds),
        out_shape=[jax.ShapeDtypeStruct(shape, kind) for kind in kinds],
        scratch_shapes=[pltpu.VMEM((3 * shape[0],) + shape[1:], jnp.bfloat16)],
        compiler_params=pltpu.CompilerParams(vmem_limit_bytes=LIMIT),
        cost_estimate=pl.CostEstimate(
            flops=2 * shape[1] * tiles.size, bytes_accessed=2 * tiles.size, transcendentals=0
        ),
        name=name,
    )(*scalars, *blocks)


def gram_kernel(scale, core_ref, mine_ref, both_ref, block_ref, part_ref, wide):
    tiles, half, width = mine_ref.shape
    core = core_ref[0, 0]
    even = core == 0
    for tile in range(tiles):
        mine, theirs = mine_ref[tile], both_ref[1 - core, (tile + tiles // 2) % tiles]
        columns = pl.ds(tile * width, width)
        wide[0:half, columns] = jnp.where(even, mine, theirs)
        wide[half : 2 * half, columns] = jnp.where(even, theirs, mine)
    block_ref[...] = wide[:, : tiles // 2 * width]
    mine = jnp.concatenate([mine_ref[tile] for tile in range(tiles)], axis=1)
    part = scale * lax.dot_general(
        mine,
        wide[...],
        (((1,), (1,)), ((), ())),
        precision=lax.Precision.HIGHEST,
        preferred_element_type=jnp.float32,
    )
    part = jnp.concatenate([part[: half // 2], part[half // 2 :]], axis=1)
    part_ref[...] = jnp.broadcast_to(part[None], part_ref.shape)


def gram_rows(core, mine, both, scale, copies):
    tiles, half, width = mine.shape
    return pl.pallas_call(
        functools.partial(gram_kernel, scale),
        in_specs=[VMEM, VMEM, VMEM],
        out_specs=[VMEM, VMEM],
        out_shape=[
            jax.ShapeDtypeStruct((2 * half, tiles // 2 * width), jnp.float32),
            jax.ShapeDtypeStruct((copies, half // 2, 4 * half), jnp.float32),
        ],
        scratch_shapes=[pltpu.VMEM((2 * half, tiles * width), jnp.float32)],
        compiler_params=pltpu.CompilerParams(vmem_limit_bytes=LIMIT),
        name="gram",
    )(core, mine, both)


def sum_kernel(parts_ref, out_ref):
    parts = [parts_ref[at] for at in range(parts_ref.shape[0])]
    while len(parts) > 1:
        parts = [one + other for one, other in zip(parts[::2], parts[1::2])]
    out_ref[...] = jnp.broadcast_to(parts[0][None], out_ref.shape)


def summed(parts, copies):
    return pl.pallas_call(
        sum_kernel,
        in_specs=[VMEM],
        out_specs=VMEM,
        out_shape=jax.ShapeDtypeStruct((copies,) + parts.shape[1:], parts.dtype),
        compiler_params=pltpu.CompilerParams(vmem_limit_bytes=LIMIT),
        name="sum_parts",
    )(parts)


def finish_kernel(gram_ref, block_ref, basis_ref, factor_ref, rows):
    size = block_ref.shape[0]
    quarter = size // 4
    lane_of = lax.broadcasted_iota(jnp.int32, (8, 2 * size), 1)
    row_of = lax.broadcasted_iota(jnp.int32, (8, 2 * size), 0)
    groups = []
    for group in range(size // 8):
        core, row = divmod(8 * group, 2 * quarter)
        part, row = divmod(row, quarter)
        stored = gram_ref[core, row : row + 8, part * size : (part + 1) * size]
        unit = (lane_of == row_of + (8 * group + size)).astype(jnp.float32)
        groups.append(jnp.concatenate([stored, unit[:, size:]], axis=1))
    def spread(value):
        return jnp.broadcast_to(value, (8, 2 * size))

    for pivot in range(0, size, 4):
        at, inner = divmod(pivot, 8)
        columns = [
            [spread(group[:, pivot + i : pivot + i + 1]) for i in range(4)] for group in groups[at:]
        ]
        lines = [spread(groups[at][inner + i : inner + i + 1, :]) for i in range(4)]
        block = [
            [spread(columns[0][j][inner + i : inner + i + 1, :]) for j in range(i + 1)] for i in range(4)
        ]
        inverses, scales = [], []
        lower = [[None] * 4 for _ in range(4)]
        for j in range(4):
            inverse = 1.0 / block[j][j]
            inverses.append(inverse)
            scales.append(lax.rsqrt(block[j][j]))
            for i in range(j + 1, 4):
                lower[i][j] = block[i][j] * inverse
            for i in range(j + 1, 4):
                for k in range(j + 1, i + 1):
                    block[i][k] = block[i][k] - lower[i][j] * block[k][j]
        for j in range(4):
            for i in range(j + 1, 4):
                lines[i] = lines[i] - lower[i][j] * lines[j]
            rows[pivot + j : pivot + j + 1, :] = (lines[j] * scales[j])[0:1]
        for group in range(at, size // 8):
            if group == at and inner == 4:
                continue
            own = columns[group - at]
            change = None
            for j in range(4):
                for i in range(j + 1, 4):
                    own[i] = own[i] - lower[i][j] * own[j]
                part = own[j] * inverses[j] * lines[j]
                change = part if change is None else change + part
            if group == at:
                change = jnp.where(row_of > inner + 3, change, 0.0)
            groups[group] = groups[group] - change
    upper = lax.broadcasted_iota(jnp.int32, (size, size), 0) <= lax.broadcasted_iota(
        jnp.int32, (size, size), 1
    )
    done = rows[...]
    factor_ref[...] = jnp.where(upper, done[:, :size], 0.0)
    inverse, middle = done[:, size:], size // 2
    for first, last in ((0, middle), (middle, size)):
        basis_ref[first:last, :] = jnp.dot(
            inverse[first:last, :last],
            block_ref[:last, :],
            precision=lax.Precision.HIGHEST,
            preferred_element_type=jnp.float32,
        )


def finish(gram, block):
    size = block.shape[0]
    return pl.pallas_call(
        finish_kernel,
        in_specs=[VMEM, VMEM],
        out_specs=[VMEM, VMEM],
        out_shape=[
            jax.ShapeDtypeStruct(block.shape, jnp.float32),
            jax.ShapeDtypeStruct((size, size), jnp.float32),
        ],
        scratch_shapes=[pltpu.VMEM((size, 2 * size), jnp.float32)],
        compiler_params=pltpu.CompilerParams(vmem_limit_bytes=LIMIT),
        name="factor_and_solve",
    )(gram, block)


def shards(start_block, operator_tiles, tile_pattern):
    vectors, node_count = start_block.shape
    rows_local, _, tile_size = operator_tiles.shape[:3]
    half = vectors // 2
    device_count = lax.axis_size(AXES)
    position = lax.axis_index(AXES)
    chip, core = position // 2, position % 2
    chip_rows = 2 * rows_local

    row_ids = jnp.arange(rows_local, dtype=jnp.int32)[:, None]
    away = tile_pattern - (position * rows_local + row_ids)
    start_tiles = start_block.reshape(vectors, rows_local, tile_size).transpose(1, 0, 2)
    low, high = start_tiles[:, :half], start_tiles[:, half:]
    slots = away.shape[1]
    packed = jnp.zeros((1, half, tile_size), jnp.bfloat16)
    packed = packed.at[0, :rows_local, :slots].set(away.astype(jnp.bfloat16))
    sent = of_both_cores(jnp.concatenate([jnp.where(core == 0, high, low), packed], axis=0))
    theirs = jnp.where(core == 0, sent[1], sent[0])
    rounded = jnp.concatenate([jnp.where(core == 0, low, high), theirs[:rows_local]], axis=0)
    far_away = theirs[rows_local, :rows_local, :slots].astype(jnp.int32)

    operator_tiles, rounded = lax.optimization_barrier((operator_tiles, rounded))
    tiles = turned(operator_tiles, swapped(operator_tiles))

    far_rows = (position ^ 1) * rows_local + row_ids
    columns = jnp.concatenate([tile_pattern, far_away + far_rows], axis=0)
    index = jnp.clip(columns - (chip - 1) * chip_rows, 0, 3 * chip_rows - 1)
    place, inner = index // chip_rows, (index % chip_rows) ^ (core * rows_local)
    index = jnp.where(chip % 2 == 1, (place + 1) % 3, place) * chip_rows + inner

    earlier = rounded.astype(jnp.float32)
    even_chip = (1 - chip % 2).reshape(1, 1)
    latest, rounded = stepped(
        first_kernel,
        "first_step",
        (index, even_chip),
        (traded(rounded, 1), rounded, traded(rounded, 0), tiles),
    )
    for degree in range(2, DEG + 1):
        keep = (degree != DEG - 1, degree != DEG)
        made = stepped(
            functools.partial(step_kernel, keep),
            "step",
            (index,),
            (paired(rounded), traded(rounded, 1), tiles, earlier),
            keep,
        )
        earlier, latest, rounded = latest, made[0], made[-1]

    inner, outer = lax.axis_size("ry") // 2, lax.axis_size("rx")
    block, parts = gram_rows(
        core.reshape(1, 1), latest, of_both_cores(latest), 1.0 / (node_count * device_count), inner
    )
    same_core = [list(range(low, 2 * inner, 2)) for low in (0, 1)]
    parts = lax.all_to_all(parts, "ry", 0, 0, axis_index_groups=same_core, tiled=True)
    parts = lax.all_to_all(summed(parts, outer), "rx", 0, 0, tiled=True)
    return tuple(finish(of_both_cores(summed(parts, 1)[0]), block))


def solution(mesh):
    return jax.shard_map(
        shards,
        mesh=mesh,
        in_specs=(P(None, AXES), P(AXES, None, None, None), P(AXES, None)),
        out_specs=(P(None, AXES), P()),
        check_vma=False,
    )
```

```python
import functools

import jax
import jax.numpy as jnp
from jax import lax
from jax.experimental import pallas as pl
from jax.experimental.pallas import tpu as pltpu
from jax.sharding import PartitionSpec as P

DEG = 12
AXES = ("rx", "ry")
VMEM = pl.BlockSpec(memory_space=pltpu.VMEM)
LIMIT = 16 * 2**20


def traded(value, first):
    count = lax.axis_size(AXES)
    route = []
    for low in range(2 * first, count - 2, 4):
        for core in (0, 1):
            route += [(low + core, low + core + 2), (low + core + 2, low + core)]
    return lax.ppermute(value, AXES, route)


def paired(value):
    groups = []
    for low in range(0, lax.axis_size("ry"), 4):
        groups += [[low, low + 2], [low + 1, low + 3]]
    return lax.all_gather(value, "ry", axis_index_groups=groups)


def of_both_cores(value):
    count = lax.axis_size("ry")
    groups = [[low, low + 1] for low in range(0, count, 2)]
    return lax.all_gather(value, "ry", axis_index_groups=groups)


def swapped(value):
    count = lax.axis_size(AXES)
    return lax.ppermute(value, AXES, [(source, source ^ 1) for source in range(count)])


def split_kernel(position_ref, start_ref, pattern_ref, mine_ref, sent_ref):
    tiles, half, width = mine_ref.shape
    position = position_ref[0, 0]
    even = position % 2 == 0
    for tile in range(tiles):
        columns = slice(tile * width, (tile + 1) * width)
        low, high = start_ref[0:half, columns], start_ref[half : 2 * half, columns]
        mine_ref[tile] = jnp.where(even, low, high)
        sent_ref[tile] = jnp.where(even, high, low)
    rows, slots = pattern_ref.shape
    row_ids = lax.broadcasted_iota(jnp.int32, (rows, slots), 0) + position * rows
    away = (pattern_ref[...] - row_ids).astype(jnp.float32)
    away = jnp.concatenate([away, jnp.zeros((rows, width - slots), jnp.float32)], axis=1)
    away = jnp.concatenate([away, jnp.zeros((half - rows, width), jnp.float32)], axis=0)
    sent_ref[tiles] = away.astype(jnp.bfloat16)


def split(position, start_block, pattern, width):
    half, tiles = start_block.shape[0] // 2, start_block.shape[1] // width
    return pl.pallas_call(
        split_kernel,
        in_specs=[VMEM, VMEM, VMEM],
        out_specs=[VMEM, VMEM],
        out_shape=[
            jax.ShapeDtypeStruct((tiles, half, width), jnp.bfloat16),
            jax.ShapeDtypeStruct((tiles + 1, half, width), jnp.bfloat16),
        ],
        compiler_params=pltpu.CompilerParams(vmem_limit_bytes=LIMIT),
        name="split_start",
    )(position, start_block, pattern)


def turn_kernel(near_ref, far_ref, out_ref):
    rows, slots = near_ref.shape[:2]
    for row in range(rows):
        for slot in range(slots):
            out_ref[row, slot] = near_ref[row, slot].T
            out_ref[rows + row, slot] = far_ref[row, slot].T


def turned(near, far):
    return pl.pallas_call(
        turn_kernel,
        in_specs=[VMEM, VMEM],
        out_specs=VMEM,
        out_shape=jax.ShapeDtypeStruct((2 * near.shape[0],) + near.shape[1:], near.dtype),
        compiler_params=pltpu.CompilerParams(vmem_limit_bytes=LIMIT),
        name="turn_tiles",
    )(near, far)


def apply_tiles(index_ref, tiles_ref, window, older_ref, latest_ref, rounded_ref):
    count, slots = tiles_ref.shape[:2]
    for row in range(count):
        total = None
        for slot in range(0, slots, 2):
            vectors = jnp.concatenate(
                [window[index_ref[row, slot]], window[index_ref[row, slot + 1]]], axis=1
            )
            tiles = jnp.concatenate([tiles_ref[row, slot], tiles_ref[row, slot + 1]], axis=0)
            part = jnp.dot(vectors, tiles, preferred_element_type=jnp.float32)
            total = part if total is None else total + part
        if older_ref is not None:
            total = 2.0 * total - older_ref[row]
        if latest_ref is not None:
            latest_ref[row] = total
        if rounded_ref is not None:
            rounded_ref[row] = total.astype(jnp.bfloat16)


def first_kernel(
    index_ref, even_chip_ref, odd_ref, own_ref, even_ref, tiles_ref, latest_ref, rounded_ref, window
):
    count = odd_ref.shape[0]
    is_even = even_chip_ref[0, 0] == 1
    own, even = own_ref[...], even_ref[...]
    window[0:count] = odd_ref[...]
    window[count : 2 * count] = jnp.where(is_even, own, even)
    window[2 * count : 3 * count] = jnp.where(is_even, even, own)
    apply_tiles(index_ref, tiles_ref, window, None, latest_ref, rounded_ref)


def step_kernel(keep, index_ref, pair_ref, odd_ref, tiles_ref, older_ref, *rest):
    latest_ref = rest[0] if keep[0] else None
    rounded_ref = rest[-2] if keep[1] else None
    window = rest[-1]
    count = odd_ref.shape[0]
    window[0:count] = odd_ref[...]
    window[count : 2 * count] = pair_ref[0]
    window[2 * count : 3 * count] = pair_ref[1]
    apply_tiles(index_ref, tiles_ref, window, older_ref, latest_ref, rounded_ref)


def stepped(kernel, name, scalars, blocks, keep=(True, True)):
    tiles = next(block for block in blocks if block.ndim == 4 and block.shape[-2] == block.shape[-1])
    shape = (tiles.shape[0], blocks[0].shape[-2], tiles.shape[2])
    kinds = [kind for kind, kept in zip((jnp.float32, jnp.bfloat16), keep) if kept]
    return pl.pallas_call(
        kernel,
        in_specs=[VMEM] * (len(scalars) + len(blocks)),
        out_specs=[VMEM] * len(kinds),
        out_shape=[jax.ShapeDtypeStruct(shape, kind) for kind in kinds],
        scratch_shapes=[pltpu.VMEM((3 * shape[0],) + shape[1:], jnp.bfloat16)],
        compiler_params=pltpu.CompilerParams(vmem_limit_bytes=LIMIT),
        cost_estimate=pl.CostEstimate(
            flops=2 * shape[1] * tiles.size, bytes_accessed=2 * tiles.size, transcendentals=0
        ),
        name=name,
    )(*scalars, *blocks)


def gram_kernel(scale, core_ref, mine_ref, both_ref, block_ref, part_ref, wide):
    tiles, half, width = mine_ref.shape
    core = core_ref[0, 0]
    even = core == 0
    for tile in range(tiles):
        mine, theirs = mine_ref[tile], both_ref[1 - core, (tile + tiles // 2) % tiles]
        columns = pl.ds(tile * width, width)
        wide[0:half, columns] = jnp.where(even, mine, theirs)
        wide[half : 2 * half, columns] = jnp.where(even, theirs, mine)
    block_ref[...] = wide[:, : tiles // 2 * width]
    mine = jnp.concatenate([mine_ref[tile] for tile in range(tiles)], axis=1)
    part = scale * lax.dot_general(
        mine,
        wide[...],
        (((1,), (1,)), ((), ())),
        precision=lax.Precision.HIGHEST,
        preferred_element_type=jnp.float32,
    )
    part = jnp.concatenate([part[: half // 2], part[half // 2 :]], axis=1)
    part_ref[...] = jnp.broadcast_to(part[None], part_ref.shape)


def gram_rows(core, mine, both, scale, copies):
    tiles, half, width = mine.shape
    return pl.pallas_call(
        functools.partial(gram_kernel, scale),
        in_specs=[VMEM, VMEM, VMEM],
        out_specs=[VMEM, VMEM],
        out_shape=[
            jax.ShapeDtypeStruct((2 * half, tiles // 2 * width), jnp.float32),
            jax.ShapeDtypeStruct((copies, half // 2, 4 * half), jnp.float32),
        ],
        scratch_shapes=[pltpu.VMEM((2 * half, tiles * width), jnp.float32)],
        compiler_params=pltpu.CompilerParams(vmem_limit_bytes=LIMIT),
        name="gram",
    )(core, mine, both)


def sum_kernel(parts_ref, out_ref):
    parts = [parts_ref[at] for at in range(parts_ref.shape[0])]
    while len(parts) > 1:
        parts = [one + other for one, other in zip(parts[::2], parts[1::2])]
    out_ref[...] = jnp.broadcast_to(parts[0][None], out_ref.shape)


def summed(parts, copies):
    return pl.pallas_call(
        sum_kernel,
        in_specs=[VMEM],
        out_specs=VMEM,
        out_shape=jax.ShapeDtypeStruct((copies,) + parts.shape[1:], parts.dtype),
        compiler_params=pltpu.CompilerParams(vmem_limit_bytes=LIMIT),
        name="sum_parts",
    )(parts)


def finish_kernel(gram_ref, block_ref, basis_ref, factor_ref, rows):
    size = block_ref.shape[0]
    quarter = size // 4
    lane_of = lax.broadcasted_iota(jnp.int32, (8, 2 * size), 1)
    row_of = lax.broadcasted_iota(jnp.int32, (8, 2 * size), 0)
    groups = []
    for group in range(size // 8):
        core, row = divmod(8 * group, 2 * quarter)
        part, row = divmod(row, quarter)
        stored = gram_ref[core, row : row + 8, part * size : (part + 1) * size]
        unit = (lane_of == row_of + (8 * group + size)).astype(jnp.float32)
        groups.append(jnp.concatenate([stored, unit[:, size:]], axis=1))
    def spread(value):
        return jnp.broadcast_to(value, (8, 2 * size))

    for pivot in range(0, size, 4):
        at, inner = divmod(pivot, 8)
        columns = [
            [spread(group[:, pivot + i : pivot + i + 1]) for i in range(4)] for group in groups[at:]
        ]
        lines = [spread(groups[at][inner + i : inner + i + 1, :]) for i in range(4)]
        block = [
            [spread(columns[0][j][inner + i : inner + i + 1, :]) for j in range(i + 1)] for i in range(4)
        ]
        inverses, scales = [], []
        lower = [[None] * 4 for _ in range(4)]
        for j in range(4):
            inverse = 1.0 / block[j][j]
            inverses.append(inverse)
            scales.append(lax.rsqrt(block[j][j]))
            for i in range(j + 1, 4):
                lower[i][j] = block[i][j] * inverse
            for i in range(j + 1, 4):
                for k in range(j + 1, i + 1):
                    block[i][k] = block[i][k] - lower[i][j] * block[k][j]
        for j in range(4):
            for i in range(j + 1, 4):
                lines[i] = lines[i] - lower[i][j] * lines[j]
            rows[pivot + j : pivot + j + 1, :] = (lines[j] * scales[j])[0:1]
        for group in range(at, size // 8):
            if group == at and inner == 4:
                continue
            own = columns[group - at]
            change = None
            for j in range(4):
                for i in range(j + 1, 4):
                    own[i] = own[i] - lower[i][j] * own[j]
                part = own[j] * inverses[j] * lines[j]
                change = part if change is None else change + part
            if group == at:
                change = jnp.where(row_of > inner + 3, change, 0.0)
            groups[group] = groups[group] - change
    upper = lax.broadcasted_iota(jnp.int32, (size, size), 0) <= lax.broadcasted_iota(
        jnp.int32, (size, size), 1
    )
    done = rows[...]
    factor_ref[...] = jnp.where(upper, done[:, :size], 0.0)
    inverse, middle = done[:, size:], size // 2
    for first, last in ((0, middle), (middle, size)):
        basis_ref[first:last, :] = jnp.dot(
            inverse[first:last, :last],
            block_ref[:last, :],
            precision=lax.Precision.HIGHEST,
            preferred_element_type=jnp.float32,
        )


def finish(gram, block):
    size = block.shape[0]
    return pl.pallas_call(
        finish_kernel,
        in_specs=[VMEM, VMEM],
        out_specs=[VMEM, VMEM],
        out_shape=[
            jax.ShapeDtypeStruct(block.shape, jnp.float32),
            jax.ShapeDtypeStruct((size, size), jnp.float32),
        ],
        scratch_shapes=[pltpu.VMEM((size, 2 * size), jnp.float32)],
        compiler_params=pltpu.CompilerParams(vmem_limit_bytes=LIMIT),
        name="factor_and_solve",
    )(gram, block)


def shards(start_block, operator_tiles, tile_pattern):
    vectors, node_count = start_block.shape
    rows_local, _, tile_size = operator_tiles.shape[:3]
    half = vectors // 2
    device_count = lax.axis_size(AXES)
    position = lax.axis_index(AXES)
    chip, core = position // 2, position % 2
    chip_rows = 2 * rows_local

    row_ids = jnp.arange(rows_local, dtype=jnp.int32)[:, None]
    slots = tile_pattern.shape[1]
    mine, sent = split(position.reshape(1, 1), start_block, tile_pattern, tile_size)
    sent = of_both_cores(sent)
    theirs = jnp.where(core == 0, sent[1], sent[0])
    rounded = jnp.concatenate([mine, theirs[:rows_local]], axis=0)
    far_away = theirs[rows_local, :rows_local, :slots].astype(jnp.int32)

    operator_tiles, rounded = lax.optimization_barrier((operator_tiles, rounded))
    tiles = turned(operator_tiles, swapped(operator_tiles))

    far_rows = (position ^ 1) * rows_local + row_ids
    columns = jnp.concatenate([tile_pattern, far_away + far_rows], axis=0)
    index = jnp.clip(columns - (chip - 1) * chip_rows, 0, 3 * chip_rows - 1)
    place, inner = index // chip_rows, (index % chip_rows) ^ (core * rows_local)
    index = jnp.where(chip % 2 == 1, (place + 1) % 3, place) * chip_rows + inner

    earlier = rounded.astype(jnp.float32)
    even_chip = (1 - chip % 2).reshape(1, 1)
    latest, rounded = stepped(
        first_kernel,
        "first_step",
        (index, even_chip),
        (traded(rounded, 1), rounded, traded(rounded, 0), tiles),
    )
    for degree in range(2, DEG + 1):
        keep = (degree != DEG - 1, degree != DEG)
        made = stepped(
            functools.partial(step_kernel, keep),
            "step",
            (index,),
            (paired(rounded), traded(rounded, 1), tiles, earlier),
            keep,
        )
        earlier, latest, rounded = latest, made[0], made[-1]

    inner, outer = lax.axis_size("ry") // 2, lax.axis_size("rx")
    block, parts = gram_rows(
        core.reshape(1, 1), latest, of_both_cores(latest), 1.0 / (node_count * device_count), inner
    )
    same_core = [list(range(low, 2 * inner, 2)) for low in (0, 1)]
    parts = lax.all_to_all(parts, "ry", 0, 0, axis_index_groups=same_core, tiled=True)
    parts = lax.all_to_all(summed(parts, outer), "rx", 0, 0, tiled=True)
    return tuple(finish(of_both_cores(summed(parts, 1)[0]), block))


def solution(mesh):
    return jax.shard_map(
        shards,
        mesh=mesh,
        in_specs=(P(None, AXES), P(AXES, None, None, None), P(AXES, None)),
        out_specs=(P(None, AXES), P()),
        check_vma=False,
    )
```
